32 devices in a mesh: lon: 4 (over x, core), lat: 4 (over z), tm: 2 (over y).
Axes of the slice: x: 2, y: 2, z: 4, core: 2. Of those that a mesh axis runs over, the one named last changes fastest.
Arguments:
- reanalysis: float32 [512, 128, 512], P('lon', 'lat', 'tm'), may hold values from 0.05 to 5
- lon_factor: float32 [64, 512], P(None, 'lon'), may hold values from 0.05 to 1
- lat_factor: float32 [64, 128], P(None, 'lat'), may hold values from 0.05 to 1
- time_factor: float32 [64, 512], P(None, 'tm'), may hold values from 0.05 to 1
Outputs:
- lon_updated: float32 [64, 512], P(None, 'lon')
- lat_updated: float32 [64, 128], P(None, 'lat')
- time_updated: float32 [64, 512], P(None, 'tm')
The draws below stay inside these ranges and needn't reach their ends.
All inputs are finite; a program needn't handle non-finite values.
Results may differ from the reference program's by a relative error of at most 0.0003.
Values sent between devices are 32-bit elements; how exact they have to be, the bound alone decides.
A program may use at most 64 MiB of HBM per device.

```python
import math
import jax
import jax.numpy as jnp
from jax import lax

RANK = 64
NLON = 512
NLAT = 128
NHR = 512


def block_scale(stream_key, shape, pieces, smallest, top_value):
    factor_of = 1.0
    for dim, blocks in pieces:
        steps = jax.random.uniform(jax.random.fold_in(jax.random.fold_in(stream_key, 6), dim), (blocks,), jnp.float32, smallest / len(pieces), top_value / len(pieces))
        factor_of = factor_of * jnp.repeat(jnp.exp(steps), shape[dim] // blocks).reshape((-1,) + (1,) * (len(shape) - 1 - dim))
    return factor_of


def setup_inputs(seed: int = 0) -> dict:
    keys = jax.random.split(jax.random.key(seed), 5)
    reanalysis = jnp.clip(jnp.exp(math.log(5.0) - 4.6051702 * jax.random.uniform(keys[0], (NLON, NLAT, NHR), jnp.float32) ** block_scale(keys[0], (NLON, NLAT, NHR), ((0, 4), (1, 4), (2, 2)), -0.2, 0.2)), 0.05, 5.0)
    lon_factor = jnp.clip(jnp.exp(math.log(1.0) - 2.9957323 * jax.random.uniform(keys[1], (RANK, NLON), jnp.float32) ** block_scale(keys[1], (RANK, NLON), ((1, 4),), -0.2, 0.2)), 0.05, 1.0)
    lat_factor = jnp.clip(jnp.exp(math.log(1.0) - 2.9957323 * jax.random.uniform(keys[2], (RANK, NLAT), jnp.float32) ** block_scale(keys[2], (RANK, NLAT), ((1, 4),), -0.2, 0.2)), 0.05, 1.0)
    time_factor = jnp.clip(jnp.exp(math.log(1.0) - 2.9957323 * jax.random.uniform(keys[3], (RANK, NHR), jnp.float32) ** block_scale(keys[3], (RANK, NHR), ((1, 2),), -0.2, 0.2)), 0.05, 1.0)
    return dict(reanalysis=reanalysis, lon_factor=lon_factor, lat_factor=lat_factor, time_factor=time_factor)


EPSILON = 1e-6


def gram_of(factor):
    return jnp.dot(factor, factor.T, precision=lax.Precision.HIGHEST)


def hals(factor, terms, gram):
    rank = factor.shape[0]

    def update(index, current):
        grow = lax.dynamic_slice_in_dim(gram, index, 1, 0)
        pivot = lax.dynamic_slice_in_dim(grow, index, 1, 1)
        row = lax.dynamic_slice_in_dim(current, index, 1, 0)
        target = lax.dynamic_slice_in_dim(terms, index, 1, 0)
        change = (target - jnp.dot(grow, current, precision=lax.Precision.HIGHEST)) / pivot
        return lax.dynamic_update_slice_in_dim(current, jnp.maximum(row + change, EPSILON), index, 0)

    return lax.fori_loop(0, rank, update, factor)


def reference(reanalysis, lon_factor, lat_factor, time_factor):
    nlon, nlat, nhr = reanalysis.shape
    rank = lon_factor.shape[0]
    flat = reanalysis.reshape(nlon * nlat, nhr)
    inner = lax.dot_general(time_factor, flat, (((1,), (1,)), ((), ())), precision=lax.Precision.HIGHEST)
    inner = inner.reshape(rank, nlon, nlat)
    lon_terms = jnp.sum(inner * lat_factor[:, None, :], axis=2)
    lon_new = hals(lon_factor, lon_terms, gram_of(lat_factor) * gram_of(time_factor))
    lat_terms = jnp.sum(inner * lon_new[:, :, None], axis=1)
    lat_new = hals(lat_factor, lat_terms, gram_of(lon_new) * gram_of(time_factor))
    pairs = (lon_new[:, :, None] * lat_new[:, None, :]).reshape(rank, nlon * nlat)
    time_terms = jnp.dot(pairs, flat, precision=lax.Precision.HIGHEST)
    time_new = hals(time_factor, time_terms, gram_of(lon_new) * gram_of(lat_new))
    return lon_new, lat_new, time_new
```

```python
import functools

import jax
import jax.numpy as jnp
from jax import lax
from jax.experimental import pallas as pl
from jax.experimental.pallas import tpu as pltpu
from jax.sharding import PartitionSpec as P

EPSILON = 1e-06
MESH = pl.DeviceIdType.MESH
SUB = 8
LANE = 128


def gram_of(factor):
    return lax.dot_general(
        factor, factor, (((1,), (1,)), ((), ())),
        precision=lax.Precision.HIGHEST, preferred_element_type=jnp.float32,
    )


def halves(value):
    high = value.astype(jnp.bfloat16)
    return high, (value - high.astype(jnp.float32)).astype(jnp.bfloat16)


def widen(value, rows, cols):
    r, c = value.shape
    if c < cols:
        value = jnp.concatenate([value, jnp.zeros((r, cols - c), value.dtype)], axis=1)
    if r < rows:
        value = jnp.concatenate([value, jnp.zeros((rows - r, cols), value.dtype)], axis=0)
    return value


def turn(value):
    r, c = value.shape
    full = widen(value, -(-r // LANE) * LANE, -(-c // LANE) * LANE)
    return full.T[:c, :r]


def hals(out_ref, factor, terms, gram):
    rank = factor.shape[0]
    row = lax.broadcasted_iota(jnp.int32, (rank, rank), 0)
    col = lax.broadcasted_iota(jnp.int32, (rank, rank), 1)
    inverse = 1.0 / jnp.sum(jnp.where(row == col, gram, 0.0), axis=1, keepdims=True)
    scaled = gram * inverse
    rest = (terms - jnp.dot(gram, factor, precision=lax.Precision.HIGHEST,
                            preferred_element_type=jnp.float32)) * inverse
    for r in range(rank):
        old = factor[r:r + 1]
        new = jnp.maximum(old + rest[r:r + 1], EPSILON)
        out_ref[r:r + 1, :] = new
        if r < rank - 1:
            rest = rest - scaled[:, r:r + 1] * (new - old)


class Group:
    def __init__(self, sizes, axes):
        self.axes = axes
        self.sizes = [sizes[a] for a in axes]
        self.count = 1
        for s in self.sizes:
            self.count *= s

    def me(self):
        index = 0
        for a, s in zip(self.axes, self.sizes):
            index = index * s + lax.axis_index(a)
        return index

    def device(self, index):
        place = {}
        for a, s in reversed(list(zip(self.axes, self.sizes))):
            place[a] = lax.rem(index, s)
            index = lax.div(index, s)
        return place

    def peer(self, offset):
        return lax.rem(self.me() + offset, self.count)

    def source(self, offset):
        return lax.rem(self.me() + (self.count - offset), self.count)


def when(condition, action):
    if condition is True:
        action()
    else:
        pl.when(condition)(action)


class Share:
    def __init__(self, group, slots, send, recv):
        self.group, self.slots = group, slots
        self.copies = []
        me = group.me()
        for o in range(1, group.count):
            self.copies.append(pltpu.make_async_remote_copy(
                src_ref=slots.at[me], dst_ref=slots.at[me],
                send_sem=send.at[o - 1], recv_sem=recv.at[o - 1],
                device_id=group.device(group.peer(o)), device_id_type=MESH))

    def start(self, value):
        self.slots[self.group.me()] = value
        for copy in self.copies:
            copy.start()

    def finish(self):
        for copy in self.copies:
            copy.wait()
        total = self.slots[0]
        for i in range(1, self.group.count):
            total = total + self.slots[i]
        return total


class Reduce:
    def __init__(self, group, part, slots, final, send1, recv1, send2, recv2):
        self.group, self.part, self.slots, self.final = group, part, slots, final
        pieces = part.shape[0]
        self.owners = min(group.count, pieces)
        self.per = pieces // self.owners
        self.all_own = self.owners == group.count
        me = group.me()
        self.scatter, self.gather = [], []
        for o in range(1, group.count):
            to = group.peer(o)
            device = group.device(to)
            self.scatter.append(pltpu.make_async_remote_copy(
                src_ref=part.at[self.tiles(to)], dst_ref=slots.at[o - 1],
                send_sem=send1.at[o - 1], recv_sem=recv1.at[o - 1],
                device_id=device, device_id_type=MESH))
            self.gather.append(pltpu.make_async_remote_copy(
                src_ref=final.at[self.tiles(me)], dst_ref=final.at[self.tiles(me)],
                send_sem=send2.at[o - 1], recv_sem=recv2.at[o - 1],
                device_id=device, device_id_type=MESH))

    def owns(self, index):
        return True if self.all_own else index < self.owners

    def tiles(self, index):
        if not self.all_own:
            index = jnp.minimum(index, self.owners - 1)
        return pl.ds(index * self.per, self.per)

    def start(self, value):
        for i in range(value.shape[1] // LANE):
            rows = value.shape[0] // SUB
            self.part[i * rows:(i + 1) * rows] = value[:, i * LANE:(i + 1) * LANE].reshape(rows, SUB, LANE)
        for o, copy in enumerate(self.scatter, 1):
            when(self.owns(self.group.peer(o)), copy.start)

    def middle(self):
        me = self.group.me()

        def add():
            for copy in self.scatter:
                copy.wait_recv()
            total = self.part[self.tiles(me)]
            for o in range(1, self.group.count):
                total = total + self.slots[o - 1]
            self.final[self.tiles(me)] = total
            for copy in self.gather:
                copy.start()

        when(self.owns(me), add)

    def finish(self, rank):
        me = self.group.me()
        for o, copy in enumerate(self.gather, 1):
            when(self.owns(self.group.source(o)), copy.wait_recv)
        rows = rank // SUB
        pieces = self.part.shape[0]
        tiles = [self.final[i:i + rows].reshape(rank, LANE) for i in range(0, pieces, rows)]
        return tiles[0] if len(tiles) == 1 else jnp.concatenate(tiles, axis=1)

    def drain(self):
        for o, copy in enumerate(self.scatter, 1):
            when(self.owns(self.group.peer(o)), copy.wait_send)

        def sent():
            for copy in self.gather:
                copy.wait_send()

        when(self.owns(self.group.me()), sent)


def kernel(sizes, shape, x_ref, lon_ref, lat_ref, time_ref, lon_out, lat_out, time_out,
           xh, xl, inner, lon_t, *comm):
    n_lon, n_lat, n_hr = shape
    rank = lon_ref.shape[0]
    lon_axis, lat_axis, tm_axis = (Group(sizes, (a,)) for a in ("lon", "lat", "tm"))
    lat_tm, lon_tm, lon_lat = Group(sizes, ("lat", "tm")), Group(sizes, ("lon", "tm")), Group(sizes, ("lon", "lat"))

    barrier = pltpu.get_barrier_semaphore()
    signals = 0
    for group in (lat_tm, lon_tm, lon_lat):
        for o in range(1, group.count):
            pl.semaphore_signal(barrier, inc=1, device_id=group.device(group.peer(o)), device_id_type=MESH)
            signals += 1
    pl.semaphore_wait(barrier, signals)

    lat_gram = Share(lat_axis, *comm[0:3])
    time_gram = Share(tm_axis, *comm[3:6])
    lon_gram = Share(lon_axis, *comm[6:9])
    lat_gram_new = Share(lat_axis, *comm[9:12])
    lon_sum = Reduce(lat_tm, *comm[12:19])
    lat_sum = Reduce(lon_tm, *comm[19:26])
    time_sum = Reduce(lon_lat, *comm[26:33])

    lat_gram.start(gram_of(lat_ref[...]))
    time_gram.start(gram_of(time_ref[...]))

    step = 16
    chunk = step * n_lat
    weights = jnp.concatenate(halves(time_ref[...]), axis=0)
    lat_t = turn(lat_ref[...])

    def first(c, _):
        rows = pl.ds(pl.multiple_of(c * chunk, chunk), chunk)
        high, low = halves(x_ref[rows, :])
        xh[rows, :] = high
        xl[rows, :] = low
        nt = (((1,), (1,)), ((), ()))
        both = lax.dot_general(high, weights, nt, preferred_element_type=jnp.float32)
        both = both + lax.dot_general(low, weights, nt, preferred_element_type=jnp.float32)
        value = both[:, :rank] + both[:, rank:]
        inner[rows, :] = value
        lon_t[pl.ds(pl.multiple_of(c * step, step), step), :] = jnp.sum(
            value.reshape(step, n_lat, rank) * lat_t[None], axis=1)
        return 0

    lax.fori_loop(0, n_lon // step, first, 0)
    lon_sum.start(turn(lon_t[...]))
    lon_sum.middle()
    time_g = time_gram.finish()
    gram = lat_gram.finish() * time_g
    hals(lon_out, lon_ref[...], lon_sum.finish(rank), gram)

    lon_new = lon_out[...]
    lon_gram.start(gram_of(lon_new))
    lon_t[...] = turn(lon_new)

    def second(c, total):
        rows = pl.ds(pl.multiple_of(c * chunk, chunk), chunk)
        scale = lon_t[pl.ds(pl.multiple_of(c * step, step), step), :]
        return total + jnp.sum(inner[rows, :].reshape(step, n_lat, rank) * scale[:, None, :], axis=0)

    lat_part = lax.fori_loop(0, n_lon // step, second, jnp.zeros((n_lat, rank), jnp.float32))
    lat_sum.start(widen(turn(lat_part), rank, -(-n_lat // LANE) * LANE))
    lat_sum.middle()
    lon_g = lon_gram.finish()
    gram = lon_g * time_g
    hals(lat_out, lat_ref[...], lat_sum.finish(rank)[:, :n_lat], gram)

    lat_new = lat_out[...]
    lat_gram_new.start(gram_of(lat_new))
    lat_t = turn(lat_new)

    def third(c, total):
        rows = pl.ds(pl.multiple_of(c * chunk, chunk), chunk)
        scale = lon_t[pl.ds(pl.multiple_of(c * step, step), step), :]
        pairs = (scale[:, None, :] * lat_t[None]).reshape(chunk, rank)
        high = pairs.astype(jnp.bfloat16).astype(jnp.float32)
        both = jnp.concatenate([high, pairs - high], axis=1).T.astype(jnp.bfloat16)
        total = total + jnp.dot(both, xh[rows, :], preferred_element_type=jnp.float32)
        return total + jnp.dot(both, xl[rows, :], preferred_element_type=jnp.float32)

    both = lax.fori_loop(0, n_lon // step, third, jnp.zeros((2 * rank, n_hr), jnp.float32))
    time_sum.start(both[:rank] + both[rank:])
    time_sum.middle()
    gram = lon_g * lat_gram_new.finish()
    hals(time_out, time_ref[...], time_sum.finish(rank), gram)
    for part in (lon_sum, lat_sum, time_sum):
        part.drain()


def shards(sizes, reanalysis, lon_factor, lat_factor, time_factor):
    n_lon, n_lat, n_hr = reanalysis.shape
    rank = lon_factor.shape[0]
    cells = n_lon * n_lat
    flat = reanalysis.reshape(cells, n_hr)

    def sems(count):
        return [pltpu.SemaphoreType.DMA((max(count - 1, 1),))] * 2

    def share(count):
        return [pltpu.VMEM((count, rank, rank), jnp.float32)] + sems(count)

    def reduce(count, columns):
        pieces = rank // SUB * -(-columns // LANE)
        per = pieces // min(count, pieces)
        return [
            pltpu.VMEM((pieces, SUB, LANE), jnp.float32),
            pltpu.VMEM((max(count - 1, 1), per, SUB, LANE), jnp.float32),
            pltpu.VMEM((pieces, SUB, LANE), jnp.float32),
        ] + sems(count) + sems(count)

    lon, lat, tm = sizes["lon"], sizes["lat"], sizes["tm"]
    comm = share(lat) + share(tm) + share(lon) + share(lat)
    comm += reduce(lat * tm, n_lon) + reduce(lon * tm, n_lat) + reduce(lon * lat, n_hr)
    return pl.pallas_call(
        functools.partial(kernel, sizes, (n_lon, n_lat, n_hr)),
        out_shape=[jax.ShapeDtypeStruct(f.shape, jnp.float32) for f in (lon_factor, lat_factor, time_factor)],
        in_specs=[pl.BlockSpec(memory_space=pltpu.VMEM)] * 4,
        out_specs=[pl.BlockSpec(memory_space=pltpu.VMEM)] * 3,
        scratch_shapes=[
            pltpu.VMEM((cells, n_hr), jnp.bfloat16),
            pltpu.VMEM((cells, n_hr), jnp.bfloat16),
            pltpu.VMEM((cells, rank), jnp.float32),
            pltpu.VMEM((n_lon, rank), jnp.float32),
        ] + comm,
        compiler_params=pltpu.CompilerParams(
            collective_id=0, has_side_effects=True, vmem_limit_bytes=40 * 1024 * 1024),
    )(flat, lon_factor, lat_factor, time_factor)


def solution(mesh):
    sizes = dict(mesh.shape)
    in_specs = (P("lon", "lat", "tm"), P(None, "lon"), P(None, "lat"), P(None, "tm"))
    out_specs = (P(None, "lon"), P(None, "lat"), P(None, "tm"))

    def run(*args):
        return tuple(shards(sizes, *args))

    return jax.shard_map(run, mesh=mesh, in_specs=in_specs, out_specs=out_specs, check_vma=False)
```

```python
import functools

import jax
import jax.numpy as jnp
from jax import lax
from jax.experimental import pallas as pl
from jax.experimental.pallas import tpu as pltpu
from jax.sharding import PartitionSpec as P

EPSILON = 1e-06
MESH = pl.DeviceIdType.MESH
SUB = 8
LANE = 128


def gram_of(factor):
    return lax.dot_general(
        factor, factor, (((1,), (1,)), ((), ())),
        precision=lax.Precision.HIGHEST, preferred_element_type=jnp.float32,
    )


def halves(value):
    high = value.astype(jnp.bfloat16)
    return high, (value - high.astype(jnp.float32)).astype(jnp.bfloat16)


def widen(value, rows, cols):
    r, c = value.shape
    if c < cols:
        value = jnp.concatenate([value, jnp.zeros((r, cols - c), value.dtype)], axis=1)
    if r < rows:
        value = jnp.concatenate([value, jnp.zeros((rows - r, cols), value.dtype)], axis=0)
    return value


def turn(value):
    r, c = value.shape
    full = widen(value, -(-r // LANE) * LANE, -(-c // LANE) * LANE)
    return full.T[:c, :r]


def hals(out_ref, factor, terms, gram):
    rank = factor.shape[0]
    row = lax.broadcasted_iota(jnp.int32, (rank, rank), 0)
    col = lax.broadcasted_iota(jnp.int32, (rank, rank), 1)
    inverse = 1.0 / jnp.sum(jnp.where(row == col, gram, 0.0), axis=1, keepdims=True)
    scaled = gram * inverse
    rest = (terms - jnp.dot(gram, factor, precision=lax.Precision.HIGHEST,
                            preferred_element_type=jnp.float32)) * inverse
    for r in range(rank):
        old = factor[r:r + 1]
        new = jnp.maximum(old + rest[r:r + 1], EPSILON)
        out_ref[r:r + 1, :] = new
        if r < rank - 1:
            rest = rest - scaled[:, r:r + 1] * (new - old)


def pack(value, lanes=LANE):
    rows, cols = value.shape
    blocks = max(lanes // cols, 1)
    step = rows // blocks
    return jnp.concatenate([value[i * step:(i + 1) * step] for i in range(blocks)], axis=1)


def unpack(value, cols):
    return jnp.concatenate([value[:, i:i + cols] for i in range(0, value.shape[1], cols)], axis=0)


class Group:
    def __init__(self, sizes, axes):
        self.axes = axes
        self.sizes = [sizes[a] for a in axes]
        self.count = 1
        for s in self.sizes:
            self.count *= s

    def me(self):
        index = 0
        for a, s in zip(self.axes, self.sizes):
            index = index * s + lax.axis_index(a)
        return index

    def device(self, index):
        place = {}
        for a, s in reversed(list(zip(self.axes, self.sizes))):
            place[a] = lax.rem(index, s)
            index = lax.div(index, s)
        return place

    def peer(self, offset):
        return lax.rem(self.me() + offset, self.count)

    def source(self, offset):
        return lax.rem(self.me() + (self.count - offset), self.count)


def when(condition, action):
    if condition is True:
        action()
    else:
        pl.when(condition)(action)


class Share:
    def __init__(self, group, slots, send, recv):
        self.group, self.slots = group, slots
        self.copies = []
        me = group.me()
        for o in range(1, group.count):
            self.copies.append(pltpu.make_async_remote_copy(
                src_ref=slots.at[me], dst_ref=slots.at[me],
                send_sem=send.at[o - 1], recv_sem=recv.at[o - 1],
                device_id=group.device(group.peer(o)), device_id_type=MESH))

    def start(self, value):
        self.slots[self.group.me()] = pack(value)
        for copy in self.copies:
            copy.start()

    def finish(self, cols):
        for copy in self.copies:
            copy.wait()
        total = self.slots[0]
        for i in range(1, self.group.count):
            total = total + self.slots[i]
        return unpack(total, cols)


class Reduce:
    def __init__(self, group, part, slots, final, send1, recv1, send2, recv2):
        self.group, self.part, self.slots, self.final = group, part, slots, final
        pieces = part.shape[0]
        self.owners = min(group.count, pieces)
        self.per = pieces // self.owners
        self.all_own = self.owners == group.count
        me = group.me()
        self.scatter, self.gather = [], []
        for o in range(1, group.count):
            to = group.peer(o)
            device = group.device(to)
            self.scatter.append(pltpu.make_async_remote_copy(
                src_ref=part.at[self.tiles(to)], dst_ref=slots.at[o - 1],
                send_sem=send1.at[o - 1], recv_sem=recv1.at[o - 1],
                device_id=device, device_id_type=MESH))
            self.gather.append(pltpu.make_async_remote_copy(
                src_ref=final.at[self.tiles(me)], dst_ref=final.at[self.tiles(me)],
                send_sem=send2.at[o - 1], recv_sem=recv2.at[o - 1],
                device_id=device, device_id_type=MESH))

    def owns(self, index):
        return True if self.all_own else index < self.owners

    def tiles(self, index):
        if not self.all_own:
            index = jnp.minimum(index, self.owners - 1)
        return pl.ds(index * self.per, self.per)

    def start(self, value):
        for i in range(value.shape[1] // LANE):
            rows = value.shape[0] // SUB
            self.part[i * rows:(i + 1) * rows] = value[:, i * LANE:(i + 1) * LANE].reshape(rows, SUB, LANE)
        for o, copy in enumerate(self.scatter, 1):
            when(self.owns(self.group.peer(o)), copy.start)

    def middle(self):
        me = self.group.me()

        def add():
            for copy in self.scatter:
                copy.wait_recv()
            total = self.part[self.tiles(me)]
            for o in range(1, self.group.count):
                total = total + self.slots[o - 1]
            self.final[self.tiles(me)] = total
            for copy in self.gather:
                copy.start()

        when(self.owns(me), add)

    def finish(self, rank):
        me = self.group.me()
        for o, copy in enumerate(self.gather, 1):
            when(self.owns(self.group.source(o)), copy.wait_recv)
        rows = rank // SUB
        pieces = self.part.shape[0]
        tiles = [self.final[i:i + rows].reshape(rank, LANE) for i in range(0, pieces, rows)]
        return tiles[0] if len(tiles) == 1 else jnp.concatenate(tiles, axis=1)

    def drain(self):
        for o, copy in enumerate(self.scatter, 1):
            when(self.owns(self.group.peer(o)), copy.wait_send)

        def sent():
            for copy in self.gather:
                copy.wait_send()

        when(self.owns(self.group.me()), sent)


def kernel(sizes, shape, x_hbm, lon_hbm, lat_hbm, time_hbm, lon_out, lat_out, time_out,
           x_ref, lon_ref, lat_ref, time_ref, load, x_load, xh, xl, inner, lon_t, lat_new_ref, *comm):
    n_lon, n_lat, n_hr = shape
    rank = lon_ref.shape[0]
    step = 16
    chunk = step * n_lat
    small = [pltpu.make_async_copy(src, dst, load.at[i]) for i, (src, dst) in enumerate(
        ((time_hbm, time_ref), (lat_hbm, lat_ref), (lon_hbm, lon_ref)))]

    def piece(c):
        rows = pl.ds(pl.multiple_of(c * chunk, chunk), chunk)
        return pltpu.make_async_copy(x_hbm.at[rows], x_ref.at[rows], x_load.at[c])

    for copy in small:
        copy.start()
    for c in range(n_lon // step):
        piece(c).start()
    lon_axis, lat_axis, tm_axis = (Group(sizes, (a,)) for a in ("lon", "lat", "tm"))
    lat_tm, lon_tm, lon_lat = Group(sizes, ("lat", "tm")), Group(sizes, ("lon", "tm")), Group(sizes, ("lon", "lat"))

    barrier = pltpu.get_barrier_semaphore()
    signals = 0
    for group in (lat_tm, lon_tm, lon_lat):
        for o in range(1, group.count):
            pl.semaphore_signal(barrier, inc=1, device_id=group.device(group.peer(o)), device_id_type=MESH)
            signals += 1

    for copy in small:
        copy.wait()

    lat_gram = Share(lat_axis, *comm[0:3])
    time_gram = Share(tm_axis, *comm[3:6])
    lon_gram = Share(lon_axis, *comm[6:9])
    lat_gram_new = Share(lat_axis, *comm[9:12])
    lon_sum = Reduce(lat_tm, *comm[12:19])
    lat_sum = Share(lon_tm, *comm[19:22])
    time_sum = Reduce(lon_lat, *comm[22:29])

    weights = jnp.concatenate(halves(time_ref[...]), axis=0)
    lat_t = lat_ref[...]
    lat_old = turn(lat_t)
    lat_start = gram_of(lat_old)
    time_start = gram_of(time_ref[...])

    def first(c, _):
        rows = pl.ds(pl.multiple_of(c * chunk, chunk), chunk)
        piece(c).wait()
        high, low = halves(x_ref[rows, :])
        xh[rows, :] = high
        xl[rows, :] = low
        nt = (((1,), (1,)), ((), ()))
        both = lax.dot_general(high, weights, nt, preferred_element_type=jnp.float32)
        both = both + lax.dot_general(low, weights, nt, preferred_element_type=jnp.float32)
        value = both[:, :rank] + both[:, rank:]
        inner[rows, :] = value
        lon_t[pl.ds(pl.multiple_of(c * step, step), step), :] = jnp.sum(
            value.reshape(step, n_lat, rank) * lat_t[None], axis=1)
        return 0

    lax.fori_loop(0, n_lon // step, first, 0)
    lon_part = turn(lon_t[...])
    if signals:
        pl.semaphore_wait(barrier, signals)
    lon_sum.start(lon_part)
    lat_gram.start(lat_start)
    time_gram.start(time_start)
    lon_sum.middle()
    time_g = time_gram.finish(rank)
    gram = lat_gram.finish(rank) * time_g
    hals(lon_out, lon_ref[...], lon_sum.finish(rank), gram)

    lon_new = lon_out[...]
    lon_gram.start(gram_of(lon_new))
    lon_t[...] = turn(lon_new)

    def second(c, total):
        rows = pl.ds(pl.multiple_of(c * chunk, chunk), chunk)
        scale = lon_t[pl.ds(pl.multiple_of(c * step, step), step), :]
        return total + jnp.sum(inner[rows, :].reshape(step, n_lat, rank) * scale[:, None, :], axis=0)

    lat_part = lax.fori_loop(0, n_lon // step, second, jnp.zeros((n_lat, rank), jnp.float32))
    lat_sum.start(turn(lat_part))
    lon_g = lon_gram.finish(rank)
    gram = lon_g * time_g
    hals(lat_new_ref, lat_old, lat_sum.finish(n_lat), gram)

    lat_new = lat_new_ref[...]
    lat_gram_new.start(gram_of(lat_new))
    lat_t = turn(lat_new)
    lat_out[...] = lat_t

    def third(c, total):
        rows = pl.ds(pl.multiple_of(c * chunk, chunk), chunk)
        scale = lon_t[pl.ds(pl.multiple_of(c * step, step), step), :]
        pairs = (scale[:, None, :] * lat_t[None]).reshape(chunk, rank)
        high = pairs.astype(jnp.bfloat16).astype(jnp.float32)
        both = jnp.concatenate([high, pairs - high], axis=1).T.astype(jnp.bfloat16)
        total = total + jnp.dot(both, xh[rows, :], preferred_element_type=jnp.float32)
        return total + jnp.dot(both, xl[rows, :], preferred_element_type=jnp.float32)

    both = lax.fori_loop(0, n_lon // step, third, jnp.zeros((2 * rank, n_hr), jnp.float32))
    time_sum.start(both[:rank] + both[rank:])
    time_sum.middle()
    gram = lon_g * lat_gram_new.finish(rank)
    hals(time_out, time_ref[...], time_sum.finish(rank), gram)
    for part in (lon_sum, time_sum):
        part.drain()


def shards(sizes, reanalysis, lon_factor, lat_factor, time_factor):
    n_lon, n_lat, n_hr = reanalysis.shape
    rank = lon_factor.shape[0]
    cells = n_lon * n_lat
    flat = reanalysis.reshape(cells, n_hr)

    def sems(count):
        return [pltpu.SemaphoreType.DMA((max(count - 1, 1),))] * 2

    def share(count, columns=rank):
        blocks = max(LANE // columns, 1)
        return [pltpu.VMEM((count, rank // blocks, blocks * columns), jnp.float32)] + sems(count)

    def reduce(count, columns):
        pieces = rank // SUB * -(-columns // LANE)
        per = pieces // min(count, pieces)
        return [
            pltpu.VMEM((pieces, SUB, LANE), jnp.float32),
            pltpu.VMEM((max(count - 1, 1), per, SUB, LANE), jnp.float32),
            pltpu.VMEM((pieces, SUB, LANE), jnp.float32),
        ] + sems(count) + sems(count)

    lon, lat, tm = sizes["lon"], sizes["lat"], sizes["tm"]
    comm = share(lat) + share(tm) + share(lon) + share(lat)
    comm += reduce(lat * tm, n_lon) + share(lon * tm, n_lat) + reduce(lon * lat, n_hr)
    lat_turned = lat_factor.T
    lon_new, lat_new, time_new = pl.pallas_call(
        functools.partial(kernel, sizes, (n_lon, n_lat, n_hr)),
        out_shape=[jax.ShapeDtypeStruct(f.shape, jnp.float32) for f in (lon_factor, lat_turned, time_factor)],
        in_specs=[pl.BlockSpec(memory_space=pltpu.HBM)] * 4,
        out_specs=[pl.BlockSpec(memory_space=pltpu.VMEM)] * 3,
        scratch_shapes=[
            pltpu.VMEM(flat.shape, jnp.float32),
            pltpu.VMEM(lon_factor.shape, jnp.float32),
            pltpu.VMEM(lat_turned.shape, jnp.float32),
            pltpu.VMEM(time_factor.shape, jnp.float32),
            pltpu.SemaphoreType.DMA((3,)),
            pltpu.SemaphoreType.DMA((n_lon // 16,)),
            pltpu.VMEM((cells, n_hr), jnp.bfloat16),
            pltpu.VMEM((cells, n_hr), jnp.bfloat16),
            pltpu.VMEM((cells, rank), jnp.float32),
            pltpu.VMEM((n_lon, rank), jnp.float32),
            pltpu.VMEM(lat_factor.shape, jnp.float32),
        ] + comm,
        compiler_params=pltpu.CompilerParams(
            collective_id=0, has_side_effects=True, vmem_limit_bytes=40 * 1024 * 1024),
    )(flat, lon_factor, lat_turned, time_factor)
    return lon_new, lat_new.T, time_new


def solution(mesh):
    sizes = dict(mesh.shape)
    in_specs = (P("lon", "lat", "tm"), P(None, "lon"), P(None, "lat"), P(None, "tm"))
    out_specs = (P(None, "lon"), P(None, "lat"), P(None, "tm"))

    def run(*args):
        return tuple(shards(sizes, *args))

    return jax.shard_map(run, mesh=mesh, in_specs=in_specs, out_specs=out_specs, check_vma=False)
```

```python
import functools

import jax
import jax.numpy as jnp
from jax import lax
from jax.experimental import pallas as pl
from jax.experimental.pallas import tpu as pltpu
from jax.sharding import PartitionSpec as P

EPSILON = 1e-06
MESH = pl.DeviceIdType.MESH
SUB = 8
LANE = 128


def gram_of(factor):
    return lax.dot_general(
        factor, factor, (((1,), (1,)), ((), ())),
        precision=lax.Precision.HIGHEST, preferred_element_type=jnp.float32,
    )


def halves(value):
    high = value.astype(jnp.bfloat16)
    return high, (value - high.astype(jnp.float32)).astype(jnp.bfloat16)


def widen(value, rows, cols):
    r, c = value.shape
    if c < cols:
        value = jnp.concatenate([value, jnp.zeros((r, cols - c), value.dtype)], axis=1)
    if r < rows:
        value = jnp.concatenate([value, jnp.zeros((rows - r, cols), value.dtype)], axis=0)
    return value


def turn(value):
    r, c = value.shape
    full = widen(value, -(-r // LANE) * LANE, -(-c // LANE) * LANE)
    return full.T[:c, :r]


def hals(out_ref, factor, terms, gram):
    rank = factor.shape[0]
    row = lax.broadcasted_iota(jnp.int32, (rank, rank), 0)
    col = lax.broadcasted_iota(jnp.int32, (rank, rank), 1)
    inverse = 1.0 / jnp.sum(jnp.where(row == col, gram, 0.0), axis=1, keepdims=True)
    scaled = gram * inverse
    rest = (terms - jnp.dot(gram, factor, precision=lax.Precision.HIGHEST,
                            preferred_element_type=jnp.float32)) * inverse
    for r in range(rank):
        old = factor[r:r + 1]
        new = jnp.maximum(old + rest[r:r + 1], EPSILON)
        out_ref[r:r + 1, :] = new
        if r < rank - 1:
            rest = rest - scaled[:, r:r + 1] * (new - old)


def pack(value, lanes=LANE):
    rows, cols = value.shape
    blocks = max(lanes // cols, 1)
    step = rows // blocks
    return jnp.concatenate([value[i * step:(i + 1) * step] for i in range(blocks)], axis=1)


def unpack(value, cols):
    return jnp.concatenate([value[:, i:i + cols] for i in range(0, value.shape[1], cols)], axis=0)


class Group:
    def __init__(self, sizes, axes):
        self.axes = axes
        self.sizes = [sizes[a] for a in axes]
        self.count = 1
        for s in self.sizes:
            self.count *= s

    def me(self):
        index = 0
        for a, s in zip(self.axes, self.sizes):
            index = index * s + lax.axis_index(a)
        return index

    def device(self, index):
        place = {}
        for a, s in reversed(list(zip(self.axes, self.sizes))):
            place[a] = lax.rem(index, s)
            index = lax.div(index, s)
        return place

    def peer(self, offset):
        return lax.rem(self.me() + offset, self.count)

    def source(self, offset):
        return lax.rem(self.me() + (self.count - offset), self.count)


class Share:
    def __init__(self, group, slots, send, recv):
        self.group, self.slots = group, slots
        self.copies = []
        me = group.me()
        for o in range(1, group.count):
            self.copies.append(pltpu.make_async_remote_copy(
                src_ref=slots.at[me], dst_ref=slots.at[me],
                send_sem=send.at[o - 1], recv_sem=recv.at[o - 1],
                device_id=group.device(group.peer(o)), device_id_type=MESH))

    def start(self, value):
        self.slots[self.group.me()] = pack(value)
        for copy in self.copies:
            copy.start()

    def finish(self, cols):
        for copy in self.copies:
            copy.wait()
        total = self.slots[0]
        for i in range(1, self.group.count):
            total = total + self.slots[i]
        return unpack(total, cols)


class Reduce:
    def __init__(self, near, far, part, slots, across, final, *sems):
        self.near, self.far = near, far
        self.part, self.slots, self.across, self.final = part, slots, across, final
        self.per = part.shape[0] // near.count
        me, here = near.me(), far.me()
        self.scatter, self.spread, self.gather = [], [], []
        for o in range(1, near.count):
            to = near.peer(o)
            device = near.device(to)
            self.scatter.append(pltpu.make_async_remote_copy(
                src_ref=part.at[self.tiles(to)], dst_ref=slots.at[o - 1],
                send_sem=sems[0].at[o - 1], recv_sem=sems[1].at[o - 1],
                device_id=device, device_id_type=MESH))
            self.gather.append(pltpu.make_async_remote_copy(
                src_ref=final.at[self.tiles(me)], dst_ref=final.at[self.tiles(me)],
                send_sem=sems[4].at[o - 1], recv_sem=sems[5].at[o - 1],
                device_id=device, device_id_type=MESH))
        for o in range(1, far.count):
            self.spread.append(pltpu.make_async_remote_copy(
                src_ref=across.at[here], dst_ref=across.at[here],
                send_sem=sems[2].at[o - 1], recv_sem=sems[3].at[o - 1],
                device_id=far.device(far.peer(o)), device_id_type=MESH))

    def tiles(self, index):
        return pl.ds(index * self.per, self.per)

    def start(self, value):
        for i in range(value.shape[1] // LANE):
            rows = value.shape[0] // SUB
            self.part[i * rows:(i + 1) * rows] = value[:, i * LANE:(i + 1) * LANE].reshape(rows, SUB, LANE)
        for copy in self.scatter:
            copy.start()

    def middle(self):
        me = self.near.me()
        for copy in self.scatter:
            copy.wait_recv()
        total = self.part[self.tiles(me)]
        for o in range(1, self.near.count):
            total = total + self.slots[o - 1]
        self.across[self.far.me()] = total
        for copy in self.spread:
            copy.start()
        for copy in self.spread:
            copy.wait_recv()
        total = self.across[0]
        for i in range(1, self.far.count):
            total = total + self.across[i]
        self.final[self.tiles(me)] = total
        for copy in self.gather:
            copy.start()

    def finish(self, rank):
        for copy in self.gather:
            copy.wait_recv()
        rows = rank // SUB
        pieces = self.part.shape[0]
        tiles = [self.final[i:i + rows].reshape(rank, LANE) for i in range(0, pieces, rows)]
        return tiles[0] if len(tiles) == 1 else jnp.concatenate(tiles, axis=1)

    def drain(self):
        for copy in self.scatter + self.spread + self.gather:
            copy.wait_send()


def kernel(sizes, shape, x_hbm, lon_hbm, lat_hbm, time_hbm, lon_out, lat_out, time_out,
           x_ref, lon_ref, lat_ref, time_ref, load, x_load, xh, xl, inner, lon_t, lat_new_ref, *comm):
    n_lon, n_lat, n_hr = shape
    rank = lon_ref.shape[0]
    step = 16
    chunk = step * n_lat
    small = [pltpu.make_async_copy(src, dst, load.at[i]) for i, (src, dst) in enumerate(
        ((time_hbm, time_ref), (lat_hbm, lat_ref), (lon_hbm, lon_ref)))]

    def piece(c):
        rows = pl.ds(pl.multiple_of(c * chunk, chunk), chunk)
        return pltpu.make_async_copy(x_hbm.at[rows], x_ref.at[rows], x_load.at[c])

    for copy in small:
        copy.start()
    for c in range(n_lon // step):
        piece(c).start()
    lon_axis, lat_axis, tm_axis = (Group(sizes, (a,)) for a in ("lon", "lat", "tm"))
    lon_tm = Group(sizes, ("lon", "tm"))

    barrier = pltpu.get_barrier_semaphore()
    signals = 0
    for group in (lon_tm, lat_axis):
        for o in range(1, group.count):
            pl.semaphore_signal(barrier, inc=1, device_id=group.device(group.peer(o)), device_id_type=MESH)
            signals += 1

    for copy in small:
        copy.wait()

    lat_gram = Share(lat_axis, *comm[0:3])
    time_gram = Share(tm_axis, *comm[3:6])
    lon_gram = Share(lon_axis, *comm[6:9])
    lat_gram_new = Share(lat_axis, *comm[9:12])
    lon_sum = Reduce(tm_axis, lat_axis, *comm[12:22])
    lat_sum = Share(lon_tm, *comm[22:25])
    time_sum = Reduce(lon_axis, lat_axis, *comm[25:35])

    weights = jnp.concatenate(halves(time_ref[...]), axis=0)
    lat_t = lat_ref[...]
    lat_old = turn(lat_t)
    lat_start = gram_of(lat_old)
    time_start = gram_of(time_ref[...])

    def first(c, _):
        rows = pl.ds(pl.multiple_of(c * chunk, chunk), chunk)
        piece(c).wait()
        high, low = halves(x_ref[rows, :])
        xh[rows, :] = high
        xl[rows, :] = low
        nt = (((1,), (1,)), ((), ()))
        both = lax.dot_general(high, weights, nt, preferred_element_type=jnp.float32)
        both = both + lax.dot_general(low, weights, nt, preferred_element_type=jnp.float32)
        value = both[:, :rank] + both[:, rank:]
        inner[rows, :] = value
        lon_t[pl.ds(pl.multiple_of(c * step, step), step), :] = jnp.sum(
            value.reshape(step, n_lat, rank) * lat_t[None], axis=1)
        return 0

    lax.fori_loop(0, n_lon // step, first, 0, unroll=2)
    lon_part = turn(lon_t[...])
    if signals:
        pl.semaphore_wait(barrier, signals)
    lon_sum.start(lon_part)
    lat_gram.start(lat_start)
    time_gram.start(time_start)
    lon_sum.middle()
    time_g = time_gram.finish(rank)
    gram = lat_gram.finish(rank) * time_g
    hals(lon_out, lon_ref[...], lon_sum.finish(rank), gram)

    lon_new = lon_out[...]
    lon_gram.start(gram_of(lon_new))
    lon_t[...] = turn(lon_new)

    def second(c, total):
        rows = pl.ds(pl.multiple_of(c * chunk, chunk), chunk)
        scale = lon_t[pl.ds(pl.multiple_of(c * step, step), step), :]
        return total + jnp.sum(inner[rows, :].reshape(step, n_lat, rank) * scale[:, None, :], axis=0)

    lat_part = lax.fori_loop(0, n_lon // step, second, jnp.zeros((n_lat, rank), jnp.float32), unroll=2)
    lat_sum.start(turn(lat_part))
    lon_g = lon_gram.finish(rank)
    gram = lon_g * time_g
    hals(lat_new_ref, lat_old, lat_sum.finish(n_lat), gram)

    lat_new = lat_new_ref[...]
    lat_gram_new.start(gram_of(lat_new))
    lat_t = turn(lat_new)
    lat_out[...] = lat_t

    def third(c, total):
        rows = pl.ds(pl.multiple_of(c * chunk, chunk), chunk)
        scale = lon_t[pl.ds(pl.multiple_of(c * step, step), step), :]
        pairs = (scale[:, None, :] * lat_t[None]).reshape(chunk, rank)
        high = pairs.astype(jnp.bfloat16).astype(jnp.float32)
        both = jnp.concatenate([high, pairs - high], axis=1).T.astype(jnp.bfloat16)
        total = total + jnp.dot(both, xh[rows, :], preferred_element_type=jnp.float32)
        return total + jnp.dot(both, xl[rows, :], preferred_element_type=jnp.float32)

    both = lax.fori_loop(0, n_lon // step, third, jnp.zeros((2 * rank, n_hr), jnp.float32), unroll=2)
    time_sum.start(both[:rank] + both[rank:])
    time_sum.middle()
    gram = lon_g * lat_gram_new.finish(rank)
    hals(time_out, time_ref[...], time_sum.finish(rank), gram)
    for part in (lon_sum, time_sum):
        part.drain()


def shards(sizes, reanalysis, lon_factor, lat_factor, time_factor):
    n_lon, n_lat, n_hr = reanalysis.shape
    rank = lon_factor.shape[0]
    cells = n_lon * n_lat
    flat = reanalysis.reshape(cells, n_hr)

    def sems(count):
        return [pltpu.SemaphoreType.DMA((max(count - 1, 1),))] * 2

    def share(count, columns=rank):
        blocks = max(LANE // columns, 1)
        return [pltpu.VMEM((count, rank // blocks, blocks * columns), jnp.float32)] + sems(count)

    def reduce(near, far, columns):
        pieces = rank // SUB * -(-columns // LANE)
        per = pieces // near
        return [
            pltpu.VMEM((pieces, SUB, LANE), jnp.float32),
            pltpu.VMEM((max(near - 1, 1), per, SUB, LANE), jnp.float32),
            pltpu.VMEM((far, per, SUB, LANE), jnp.float32),
            pltpu.VMEM((pieces, SUB, LANE), jnp.float32),
        ] + sems(near) + sems(far) + sems(near)

    lon, lat, tm = sizes["lon"], sizes["lat"], sizes["tm"]
    comm = share(lat) + share(tm) + share(lon) + share(lat)
    comm += reduce(tm, lat, n_lon) + share(lon * tm, n_lat) + reduce(lon, lat, n_hr)
    lat_turned = lat_factor.T
    lon_new, lat_new, time_new = pl.pallas_call(
        functools.partial(kernel, sizes, (n_lon, n_lat, n_hr)),
        out_shape=[jax.ShapeDtypeStruct(f.shape, jnp.float32) for f in (lon_factor, lat_turned, time_factor)],
        in_specs=[pl.BlockSpec(memory_space=pltpu.HBM)] * 4,
        out_specs=[pl.BlockSpec(memory_space=pltpu.VMEM)] * 3,
        scratch_shapes=[
            pltpu.VMEM(flat.shape, jnp.float32),
            pltpu.VMEM(lon_factor.shape, jnp.float32),
            pltpu.VMEM(lat_turned.shape, jnp.float32),
            pltpu.VMEM(time_factor.shape, jnp.float32),
            pltpu.SemaphoreType.DMA((3,)),
            pltpu.SemaphoreType.DMA((n_lon // 16,)),
            pltpu.VMEM((cells, n_hr), jnp.bfloat16),
            pltpu.VMEM((cells, n_hr), jnp.bfloat16),
            pltpu.VMEM((cells, rank), jnp.float32),
            pltpu.VMEM((n_lon, rank), jnp.float32),
            pltpu.VMEM(lat_factor.shape, jnp.float32),
        ] + comm,
        compiler_params=pltpu.CompilerParams(
            collective_id=0, has_side_effects=True, vmem_limit_bytes=63 * 1024 * 1024),
    )(flat, lon_factor, lat_turned, time_factor)
    return lon_new, lat_new.T, time_new


def solution(mesh):
    sizes = dict(mesh.shape)
    in_specs = (P("lon", "lat", "tm"), P(None, "lon"), P(None, "lat"), P(None, "tm"))
    out_specs = (P(None, "lon"), P(None, "lat"), P(None, "tm"))

    def run(*args):
        return tuple(shards(sizes, *args))

    return jax.shard_map(run, mesh=mesh, in_specs=in_specs, out_specs=out_specs, check_vma=False)
```

```python
import functools

import jax
import jax.numpy as jnp
from jax import lax
from jax.experimental import pallas as pl
from jax.experimental.pallas import tpu as pltpu
from jax.sharding import PartitionSpec as P

EPSILON = 1e-06
MESH = pl.DeviceIdType.MESH
SUB = 8
LANE = 128


def gram_of(factor):
    return lax.dot_general(
        factor, factor, (((1,), (1,)), ((), ())),
        precision=lax.Precision.HIGHEST, preferred_element_type=jnp.float32,
    )


def halves(value):
    high = value.astype(jnp.bfloat16)
    return high, (value - high.astype(jnp.float32)).astype(jnp.bfloat16)


def widen(value, rows, cols):
    r, c = value.shape
    if c < cols:
        value = jnp.concatenate([value, jnp.zeros((r, cols - c), value.dtype)], axis=1)
    if r < rows:
        value = jnp.concatenate([value, jnp.zeros((rows - r, cols), value.dtype)], axis=0)
    return value


def turn(value):
    r, c = value.shape
    full = widen(value, -(-r // LANE) * LANE, -(-c // LANE) * LANE)
    return full.T[:c, :r]


def hals(out_ref, factor, terms, gram):
    rank = factor.shape[0]
    row = lax.broadcasted_iota(jnp.int32, (rank, rank), 0)
    col = lax.broadcasted_iota(jnp.int32, (rank, rank), 1)
    inverse = 1.0 / jnp.sum(jnp.where(row == col, gram, 0.0), axis=1, keepdims=True)
    scaled = gram * inverse
    rest = (terms - jnp.dot(gram, factor, precision=lax.Precision.HIGHEST,
                            preferred_element_type=jnp.float32)) * inverse
    for r in range(rank):
        old = factor[r:r + 1]
        new = jnp.maximum(old + rest[r:r + 1], EPSILON)
        out_ref[r:r + 1, :] = new
        if r < rank - 1:
            rest = rest - scaled[:, r:r + 1] * (new - old)


def pack(value, lanes=LANE):
    rows, cols = value.shape
    blocks = max(lanes // cols, 1)
    step = rows // blocks
    return jnp.concatenate([value[i * step:(i + 1) * step] for i in range(blocks)], axis=1)


def unpack(value, cols):
    return jnp.concatenate([value[:, i:i + cols] for i in range(0, value.shape[1], cols)], axis=0)


class Group:
    def __init__(self, sizes, axes):
        self.axes = axes
        self.sizes = [sizes[a] for a in axes]
        self.count = 1
        for s in self.sizes:
            self.count *= s

    def me(self):
        index = 0
        for a, s in zip(self.axes, self.sizes):
            index = index * s + lax.axis_index(a)
        return index

    def device(self, index):
        place = {}
        for a, s in reversed(list(zip(self.axes, self.sizes))):
            place[a] = lax.rem(index, s)
            index = lax.div(index, s)
        return place

    def peer(self, offset):
        return lax.rem(self.me() + offset, self.count)

    def source(self, offset):
        return lax.rem(self.me() + (self.count - offset), self.count)


class Share:
    def __init__(self, group, slots, send, recv):
        self.group, self.slots = group, slots
        self.copies = []
        me = group.me()
        for o in range(1, group.count):
            self.copies.append(pltpu.make_async_remote_copy(
                src_ref=slots.at[me], dst_ref=slots.at[me],
                send_sem=send.at[o - 1], recv_sem=recv.at[o - 1],
                device_id=group.device(group.peer(o)), device_id_type=MESH))

    def start(self, value):
        self.slots[self.group.me()] = pack(value)
        for copy in self.copies:
            copy.start()

    def finish(self, cols):
        for copy in self.copies:
            copy.wait()
        total = self.slots[0]
        for i in range(1, self.group.count):
            total = total + self.slots[i]
        return unpack(total, cols)


class Reduce:
    def __init__(self, near, far, part, slots, across, final, *sems):
        self.near, self.far = near, far
        self.part, self.slots, self.across, self.final = part, slots, across, final
        self.per = part.shape[0] // near.count
        me, here = near.me(), far.me()
        self.scatter, self.spread, self.gather = [], [], []
        for o in range(1, near.count):
            to = near.peer(o)
            device = near.device(to)
            self.scatter.append(pltpu.make_async_remote_copy(
                src_ref=part.at[self.tiles(to)], dst_ref=slots.at[o - 1],
                send_sem=sems[0].at[o - 1], recv_sem=sems[1].at[o - 1],
                device_id=device, device_id_type=MESH))
            self.gather.append(pltpu.make_async_remote_copy(
                src_ref=final.at[self.tiles(me)], dst_ref=final.at[self.tiles(me)],
                send_sem=sems[4].at[o - 1], recv_sem=sems[5].at[o - 1],
                device_id=device, device_id_type=MESH))
        for o in range(1, far.count):
            self.spread.append(pltpu.make_async_remote_copy(
                src_ref=across.at[here], dst_ref=across.at[here],
                send_sem=sems[2].at[o - 1], recv_sem=sems[3].at[o - 1],
                device_id=far.device(far.peer(o)), device_id_type=MESH))

    def tiles(self, index):
        return pl.ds(index * self.per, self.per)

    def start(self, value):
        for i in range(value.shape[1] // LANE):
            rows = value.shape[0] // SUB
            self.part[i * rows:(i + 1) * rows] = value[:, i * LANE:(i + 1) * LANE].reshape(rows, SUB, LANE)
        for copy in self.scatter:
            copy.start()

    def middle(self):
        me = self.near.me()
        for copy in self.scatter:
            copy.wait_recv()
        total = self.part[self.tiles(me)]
        for o in range(1, self.near.count):
            total = total + self.slots[o - 1]
        self.across[self.far.me()] = total
        for copy in self.spread:
            copy.start()
        for copy in self.spread:
            copy.wait_recv()
        total = self.across[0]
        for i in range(1, self.far.count):
            total = total + self.across[i]
        self.final[self.tiles(me)] = total
        for copy in self.gather:
            copy.start()

    def finish(self, rank):
        for copy in self.gather:
            copy.wait_recv()
        rows = rank // SUB
        pieces = self.part.shape[0]
        tiles = [self.final[i:i + rows].reshape(rank, LANE) for i in range(0, pieces, rows)]
        return tiles[0] if len(tiles) == 1 else jnp.concatenate(tiles, axis=1)

    def drain(self):
        for copy in self.scatter + self.spread + self.gather:
            copy.wait_send()


def kernel(sizes, shape, x_hbm, lon_hbm, lat_hbm, time_hbm, lon_out, lat_out, time_out,
           lon_ref, lat_ref, time_ref, load, x_load, across, inner, lon_t, lat_new_ref, *rest):
    n_lon, n_lat, n_hr = shape
    rank = lon_ref.shape[0]
    lanes = n_hr // LANE
    x_tiles, comm = rest[:lanes], rest[lanes:]
    step = 16
    chunk = step * n_lat
    small = [pltpu.make_async_copy(src, dst, load.at[i]) for i, (src, dst) in enumerate(
        ((time_hbm, time_ref), (lat_hbm, lat_ref), (lon_hbm, lon_ref)))]

    def piece(c):
        rows = pl.ds(pl.multiple_of(c * chunk, chunk), chunk)
        return [pltpu.make_async_copy(x_hbm.at[rows, pl.ds(t * LANE, LANE)], tile.at[rows], x_load.at[t, c])
                for t, tile in enumerate(x_tiles)]

    for copy in small:
        copy.start()
    for c in range(n_lon // step):
        for copy in piece(c):
            copy.start()
    lon_axis, lat_axis, tm_axis = (Group(sizes, (a,)) for a in ("lon", "lat", "tm"))
    lon_tm = Group(sizes, ("lon", "tm"))

    barrier = pltpu.get_barrier_semaphore()
    signals = 0
    for group in (lon_tm, lat_axis):
        for o in range(1, group.count):
            pl.semaphore_signal(barrier, inc=1, device_id=group.device(group.peer(o)), device_id_type=MESH)
            signals += 1

    for copy in small:
        copy.wait()

    lat_gram = Share(lat_axis, *comm[0:3])
    time_gram = Share(tm_axis, *comm[3:6])
    lon_gram = Share(lon_axis, *comm[6:9])
    lat_gram_new = Share(lat_axis, *comm[9:12])
    lon_sum = Reduce(tm_axis, lat_axis, *comm[12:22])
    lat_sum = Share(lon_tm, *comm[22:25])
    time_sum = Reduce(lon_axis, lat_axis, *comm[25:35])

    weights = jnp.concatenate(halves(time_ref[...]), axis=0)
    lat_t = lat_ref[...]
    lat_old = turn(lat_t)
    lat_start = gram_of(lat_old)
    time_start = gram_of(time_ref[...])

    def first(c, _):
        rows = pl.ds(pl.multiple_of(c * chunk, chunk), chunk)
        for copy in piece(c):
            copy.wait()
        high, low = halves(jnp.concatenate([tile[rows, :] for tile in x_tiles], axis=1))
        nt = (((1,), (1,)), ((), ()))
        both = lax.dot_general(high, weights, nt, preferred_element_type=jnp.float32)
        both = both + lax.dot_general(low, weights, nt, preferred_element_type=jnp.float32)
        value = both[:, :rank] + both[:, rank:]
        inner[rows, :] = value
        lon_t[pl.ds(pl.multiple_of(c * step, step), step), :] = jnp.sum(
            value.reshape(step, n_lat, rank) * lat_t[None], axis=1)
        return 0

    lax.fori_loop(0, n_lon // step, first, 0, unroll=2)
    lon_part = turn(lon_t[...])
    if signals:
        pl.semaphore_wait(barrier, signals)
    lon_sum.start(lon_part)
    lat_gram.start(lat_start)
    time_gram.start(time_start)
    lon_sum.middle()
    time_g = time_gram.finish(rank)
    gram = lat_gram.finish(rank) * time_g
    hals(lon_out, lon_ref[...], lon_sum.finish(rank), gram)

    lon_new = lon_out[...]
    lon_gram.start(gram_of(lon_new))
    lon_t[...] = turn(lon_new)

    def second(c, total):
        rows = pl.ds(pl.multiple_of(c * chunk, chunk), chunk)
        scale = lon_t[pl.ds(pl.multiple_of(c * step, step), step), :]
        return total + jnp.sum(inner[rows, :].reshape(step, n_lat, rank) * scale[:, None, :], axis=0)

    lat_part = lax.fori_loop(0, n_lon // step, second, jnp.zeros((n_lat, rank), jnp.float32), unroll=2)
    lat_sum.start(turn(lat_part))

    lon_halves = jnp.concatenate(halves(lon_new), axis=0)

    def third(j, _):
        plane = jnp.concatenate(
            [tile[pl.ds(j, n_lon, stride=n_lat), :] for tile in x_tiles], axis=1)
        high, low = halves(plane)
        both = jnp.dot(lon_halves, high, preferred_element_type=jnp.float32)
        both = both + jnp.dot(lon_halves, low, preferred_element_type=jnp.float32)
        across[j] = both[:rank] + both[rank:]
        return 0

    lax.fori_loop(0, n_lat, third, 0, unroll=2)
    lon_g = lon_gram.finish(rank)
    gram = lon_g * time_g
    hals(lat_new_ref, lat_old, lat_sum.finish(n_lat), gram)

    lat_new = lat_new_ref[...]
    lat_gram_new.start(gram_of(lat_new))

    time_part = across[0] * lat_new[:, 0:1]
    for j in range(1, n_lat):
        time_part = time_part + across[j] * lat_new[:, j:j + 1]
    time_sum.start(time_part)
    time_sum.middle()
    gram = lon_g * lat_gram_new.finish(rank)
    lat_out[...] = turn(lat_new)
    hals(time_out, time_ref[...], time_sum.finish(rank), gram)
    for part in (lon_sum, time_sum):
        part.drain()


def shards(sizes, reanalysis, lon_factor, lat_factor, time_factor):
    n_lon, n_lat, n_hr = reanalysis.shape
    rank = lon_factor.shape[0]
    cells = n_lon * n_lat
    flat = reanalysis.reshape(cells, n_hr)

    def sems(count):
        return [pltpu.SemaphoreType.DMA((max(count - 1, 1),))] * 2

    def share(count, columns=rank):
        blocks = max(LANE // columns, 1)
        return [pltpu.VMEM((count, rank // blocks, blocks * columns), jnp.float32)] + sems(count)

    def reduce(near, far, columns):
        pieces = rank // SUB * -(-columns // LANE)
        per = pieces // near
        return [
            pltpu.VMEM((pieces, SUB, LANE), jnp.float32),
            pltpu.VMEM((max(near - 1, 1), per, SUB, LANE), jnp.float32),
            pltpu.VMEM((far, per, SUB, LANE), jnp.float32),
            pltpu.VMEM((pieces, SUB, LANE), jnp.float32),
        ] + sems(near) + sems(far) + sems(near)

    lon, lat, tm = sizes["lon"], sizes["lat"], sizes["tm"]
    comm = share(lat) + share(tm) + share(lon) + share(lat)
    comm += reduce(tm, lat, n_lon) + share(lon * tm, n_lat) + reduce(lon, lat, n_hr)
    lat_turned = lat_factor.T
    lon_new, lat_new, time_new = pl.pallas_call(
        functools.partial(kernel, sizes, (n_lon, n_lat, n_hr)),
        out_shape=[jax.ShapeDtypeStruct(f.shape, jnp.float32) for f in (lon_factor, lat_turned, time_factor)],
        in_specs=[pl.BlockSpec(memory_space=pltpu.HBM)] * 4,
        out_specs=[pl.BlockSpec(memory_space=pltpu.VMEM)] * 3,
        scratch_shapes=[
            pltpu.VMEM(lon_factor.shape, jnp.float32),
            pltpu.VMEM(lat_turned.shape, jnp.float32),
            pltpu.VMEM(time_factor.shape, jnp.float32),
            pltpu.SemaphoreType.DMA((3,)),
            pltpu.SemaphoreType.DMA((n_hr // LANE, n_lon // 16)),
            pltpu.VMEM((n_lat, rank, n_hr), jnp.float32),
            pltpu.VMEM((cells, rank), jnp.float32),
            pltpu.VMEM((n_lon, rank), jnp.float32),
            pltpu.VMEM(lat_factor.shape, jnp.float32),
        ] + [pltpu.VMEM((cells, LANE), jnp.float32)] * (n_hr // LANE) + comm,
        compiler_params=pltpu.CompilerParams(
            collective_id=0, has_side_effects=True, vmem_limit_bytes=61 * 1024 * 1024),
    )(flat, lon_factor, lat_turned, time_factor)
    return lon_new, lat_new.T, time_new


def solution(mesh):
    sizes = dict(mesh.shape)
    in_specs = (P("lon", "lat", "tm"), P(None, "lon"), P(None, "lat"), P(None, "tm"))
    out_specs = (P(None, "lon"), P(None, "lat"), P(None, "tm"))

    def run(*args):
        return tuple(shards(sizes, *args))

    return jax.shard_map(run, mesh=mesh, in_specs=in_specs, out_specs=out_specs, check_vma=False)
```

```python
import functools

import jax
import jax.numpy as jnp
from jax import lax
from jax.experimental import pallas as pl
from jax.experimental.pallas import tpu as pltpu
from jax.sharding import PartitionSpec as P

EPSILON = 1e-06
MESH = pl.DeviceIdType.MESH
SUB = 8
LANE = 128


def gram_of(factor):
    return lax.dot_general(
        factor, factor, (((1,), (1,)), ((), ())),
        precision=lax.Precision.HIGHEST, preferred_element_type=jnp.float32,
    )


def halves(value):
    high = value.astype(jnp.bfloat16)
    return high, (value - high.astype(jnp.float32)).astype(jnp.bfloat16)


def widen(value, rows, cols):
    r, c = value.shape
    if c < cols:
        value = jnp.concatenate([value, jnp.zeros((r, cols - c), value.dtype)], axis=1)
    if r < rows:
        value = jnp.concatenate([value, jnp.zeros((rows - r, cols), value.dtype)], axis=0)
    return value


def turn(value):
    r, c = value.shape
    full = widen(value, -(-r // LANE) * LANE, -(-c // LANE) * LANE)
    return full.T[:c, :r]


def hals(out_ref, factor, terms, gram):
    rank = factor.shape[0]
    row = lax.broadcasted_iota(jnp.int32, (rank, rank), 0)
    col = lax.broadcasted_iota(jnp.int32, (rank, rank), 1)
    inverse = 1.0 / jnp.sum(jnp.where(row == col, gram, 0.0), axis=1, keepdims=True)
    scaled = gram * inverse
    rest = (terms - jnp.dot(gram, factor, precision=lax.Precision.HIGHEST,
                            preferred_element_type=jnp.float32)) * inverse
    for r in range(rank):
        old = factor[r:r + 1]
        new = jnp.maximum(old + rest[r:r + 1], EPSILON)
        out_ref[r:r + 1, :] = new
        if r < rank - 1:
            rest = rest - scaled[:, r:r + 1] * (new - old)


def pack(value, lanes=LANE):
    rows, cols = value.shape
    blocks = max(lanes // cols, 1)
    step = rows // blocks
    return jnp.concatenate([value[i * step:(i + 1) * step] for i in range(blocks)], axis=1)


def unpack(value, cols):
    return jnp.concatenate([value[:, i:i + cols] for i in range(0, value.shape[1], cols)], axis=0)


class Group:
    def __init__(self, sizes, axes):
        self.axes = axes
        self.sizes = [sizes[a] for a in axes]
        self.count = 1
        for s in self.sizes:
            self.count *= s

    def me(self):
        index = 0
        for a, s in zip(self.axes, self.sizes):
            index = index * s + lax.axis_index(a)
        return index

    def device(self, index):
        place = {}
        for a, s in reversed(list(zip(self.axes, self.sizes))):
            place[a] = lax.rem(index, s)
            index = lax.div(index, s)
        return place

    def peer(self, offset):
        return lax.rem(self.me() + offset, self.count)

    def source(self, offset):
        return lax.rem(self.me() + (self.count - offset), self.count)


class Share:
    def __init__(self, group, slots, send, recv):
        self.group, self.slots = group, slots
        self.copies = []
        me = group.me()
        for o in range(1, group.count):
            self.copies.append(pltpu.make_async_remote_copy(
                src_ref=slots.at[me], dst_ref=slots.at[me],
                send_sem=send.at[o - 1], recv_sem=recv.at[o - 1],
                device_id=group.device(group.peer(o)), device_id_type=MESH))

    def start(self, value):
        self.slots[self.group.me()] = pack(value)
        for copy in self.copies:
            copy.start()

    def finish(self, cols):
        for copy in self.copies:
            copy.wait()
        total = self.slots[0]
        for i in range(1, self.group.count):
            total = total + self.slots[i]
        return unpack(total, cols)


class Reduce:
    def __init__(self, near, far, part, slots, across, final, *sems):
        self.near, self.far = near, far
        self.part, self.slots, self.across, self.final = part, slots, across, final
        self.per = part.shape[0] // near.count
        me, here = near.me(), far.me()
        self.scatter, self.spread, self.gather = [], [], []
        for o in range(1, near.count):
            to = near.peer(o)
            device = near.device(to)
            self.scatter.append(pltpu.make_async_remote_copy(
                src_ref=part.at[self.tiles(to)], dst_ref=slots.at[o - 1],
                send_sem=sems[0].at[o - 1], recv_sem=sems[1].at[o - 1],
                device_id=device, device_id_type=MESH))
            self.gather.append(pltpu.make_async_remote_copy(
                src_ref=final.at[self.tiles(me)], dst_ref=final.at[self.tiles(me)],
                send_sem=sems[4].at[o - 1], recv_sem=sems[5].at[o - 1],
                device_id=device, device_id_type=MESH))
        for o in range(1, far.count):
            self.spread.append(pltpu.make_async_remote_copy(
                src_ref=across.at[here], dst_ref=across.at[here],
                send_sem=sems[2].at[o - 1], recv_sem=sems[3].at[o - 1],
                device_id=far.device(far.peer(o)), device_id_type=MESH))

    def tiles(self, index):
        return pl.ds(index * self.per, self.per)

    def start(self, value):
        for i in range(value.shape[1] // LANE):
            rows = value.shape[0] // SUB
            self.part[i * rows:(i + 1) * rows] = value[:, i * LANE:(i + 1) * LANE].reshape(rows, SUB, LANE)
        for copy in self.scatter:
            copy.start()

    def middle(self):
        me = self.near.me()
        for copy in self.scatter:
            copy.wait_recv()
        total = self.part[self.tiles(me)]
        for o in range(1, self.near.count):
            total = total + self.slots[o - 1]
        self.across[self.far.me()] = total
        for copy in self.spread:
            copy.start()
        for copy in self.spread:
            copy.wait_recv()
        total = self.across[0]
        for i in range(1, self.far.count):
            total = total + self.across[i]
        self.final[self.tiles(me)] = total
        for copy in self.gather:
            copy.start()

    def finish(self, rank):
        for copy in self.gather:
            copy.wait_recv()
        rows = rank // SUB
        pieces = self.part.shape[0]
        tiles = [self.final[i:i + rows].reshape(rank, LANE) for i in range(0, pieces, rows)]
        return tiles[0] if len(tiles) == 1 else jnp.concatenate(tiles, axis=1)

    def drain(self):
        for copy in self.scatter + self.spread + self.gather:
            copy.wait_send()


def kernel(sizes, shape, x_hbm, lon_hbm, lat_hbm, time_hbm, lon_out, lat_out, time_out,
           lon_ref, lat_ref, time_ref, load, x_load, across, inner, lon_t, lat_new_ref, *rest):
    n_lon, n_lat, n_hr = shape
    rank = lon_ref.shape[0]
    lanes = n_hr // LANE
    x_tiles, comm = rest[:lanes], rest[lanes:]
    step = 16
    chunk = step * n_lat
    small = [pltpu.make_async_copy(src, dst, load.at[i]) for i, (src, dst) in enumerate(
        ((time_hbm, time_ref), (lat_hbm, lat_ref), (lon_hbm, lon_ref)))]

    def piece(c):
        rows = pl.ds(pl.multiple_of(c * chunk, chunk), chunk)
        return [pltpu.make_async_copy(x_hbm.at[rows, pl.ds(t * LANE, LANE)], tile.at[rows], x_load.at[t, c])
                for t, tile in enumerate(x_tiles)]

    for copy in small:
        copy.start()
    for c in range(n_lon // step):
        for copy in piece(c):
            copy.start()
    lon_axis, lat_axis, tm_axis = (Group(sizes, (a,)) for a in ("lon", "lat", "tm"))
    lon_tm = Group(sizes, ("lon", "tm"))

    barrier = pltpu.get_barrier_semaphore()
    signals = 0
    for group in (lon_tm, lat_axis):
        for o in range(1, group.count):
            pl.semaphore_signal(barrier, inc=1, device_id=group.device(group.peer(o)), device_id_type=MESH)
            signals += 1

    for copy in small:
        copy.wait()

    lat_gram = Share(lat_axis, *comm[0:3])
    time_gram = Share(tm_axis, *comm[3:6])
    lon_gram = Share(lon_axis, *comm[6:9])
    lat_gram_new = Share(lat_axis, *comm[9:12])
    lon_sum = Reduce(tm_axis, lat_axis, *comm[12:22])
    lat_sum = Share(lon_tm, *comm[22:25])
    time_sum = Reduce(lon_axis, lat_axis, *comm[25:35])

    weights = jnp.concatenate(halves(time_ref[...]), axis=0)
    lat_t = lat_ref[...]
    lat_old = turn(lat_t)
    lat_start = gram_of(lat_old)
    time_start = gram_of(time_ref[...])

    def first(c, _):
        rows = pl.ds(pl.multiple_of(c * chunk, chunk), chunk)
        for copy in piece(c):
            copy.wait()
        high, low = halves(jnp.concatenate([tile[rows, :] for tile in x_tiles], axis=1))
        nt = (((1,), (1,)), ((), ()))
        both = lax.dot_general(high, weights, nt, preferred_element_type=jnp.float32)
        both = both + lax.dot_general(low, weights, nt, preferred_element_type=jnp.float32)
        value = both[:, :rank] + both[:, rank:]
        inner[rows, :] = value
        lon_t[pl.ds(pl.multiple_of(c * step, step), step), :] = jnp.sum(
            value.reshape(step, n_lat, rank) * lat_t[None], axis=1)
        return 0

    lax.fori_loop(0, n_lon // step, first, 0, unroll=2)
    lon_part = turn(lon_t[...])
    if signals:
        pl.semaphore_wait(barrier, signals)
    lon_sum.start(lon_part)
    lat_gram.start(lat_start)
    time_gram.start(time_start)
    lon_sum.middle()
    time_g = time_gram.finish(rank)
    gram = lat_gram.finish(rank) * time_g
    hals(lon_out, lon_ref[...], lon_sum.finish(rank), gram)

    lon_new = lon_out[...]
    lon_gram.start(gram_of(lon_new))
    lon_t[...] = turn(lon_new)

    def second(c, total):
        rows = pl.ds(pl.multiple_of(c * chunk, chunk), chunk)
        scale = lon_t[pl.ds(pl.multiple_of(c * step, step), step), :]
        return total + jnp.sum(inner[rows, :].reshape(step, n_lat, rank) * scale[:, None, :], axis=0)

    lat_part = lax.fori_loop(0, n_lon // step, second, jnp.zeros((n_lat, rank), jnp.float32), unroll=2)
    lat_sum.start(turn(lat_part))

    lon_halves = jnp.concatenate(halves(lon_new), axis=0)

    def third(j, _):
        plane = jnp.concatenate(
            [tile[pl.ds(j, n_lon, stride=n_lat), :] for tile in x_tiles], axis=1)
        high, low = halves(plane)
        both = jnp.dot(lon_halves, high, preferred_element_type=jnp.float32)
        both = both + jnp.dot(lon_halves, low, preferred_element_type=jnp.float32)
        across[j] = both[:rank] + both[rank:]
        return 0

    lax.fori_loop(0, n_lat, third, 0, unroll=2)
    lon_g = lon_gram.finish(rank)
    gram = lon_g * time_g
    hals(lat_new_ref, lat_old, lat_sum.finish(n_lat), gram)

    lat_new = lat_new_ref[...]
    lat_gram_new.start(gram_of(lat_new))

    time_part = across[0] * lat_new[:, 0:1]
    for j in range(1, n_lat):
        time_part = time_part + across[j] * lat_new[:, j:j + 1]
    time_sum.start(time_part)
    time_sum.middle()
    gram = lon_g * lat_gram_new.finish(rank)
    lat_out[...] = turn(lat_new)
    hals(time_out, time_ref[...], time_sum.finish(rank), gram)
    for part in (lon_sum, time_sum):
        part.drain()


def shards(sizes, reanalysis, lon_factor, lat_factor, time_factor):
    n_lon, n_lat, n_hr = reanalysis.shape
    rank = lon_factor.shape[0]
    cells = n_lon * n_lat
    flat = reanalysis.reshape(cells, n_hr)

    def sems(count):
        return [pltpu.SemaphoreType.DMA((max(count - 1, 1),))] * 2

    def share(count, columns=rank):
        blocks = max(LANE // columns, 1)
        return [pltpu.VMEM((count, rank // blocks, blocks * columns), jnp.float32)] + sems(count)

    def reduce(near, far, columns):
        pieces = rank // SUB * -(-columns // LANE)
        per = pieces // near
        return [
            pltpu.VMEM((pieces, SUB, LANE), jnp.float32),
            pltpu.VMEM((max(near - 1, 1), per, SUB, LANE), jnp.float32),
            pltpu.VMEM((far, per, SUB, LANE), jnp.float32),
            pltpu.VMEM((pieces, SUB, LANE), jnp.float32),
        ] + sems(near) + sems(far) + sems(near)

    lon, lat, tm = sizes["lon"], sizes["lat"], sizes["tm"]
    comm = share(lat) + share(tm) + share(lon) + share(lat)
    comm += reduce(tm, lat, n_lon) + share(lon * tm, n_lat) + reduce(lon, lat, n_hr)
    lat_turned = lat_factor.T
    lon_new, lat_new, time_new = pl.pallas_call(
        functools.partial(kernel, sizes, (n_lon, n_lat, n_hr)),
        out_shape=[jax.ShapeDtypeStruct(f.shape, jnp.float32) for f in (lon_factor, lat_turned, time_factor)],
        in_specs=[pl.BlockSpec(memory_space=pltpu.HBM)] * 4,
        out_specs=[pl.BlockSpec(memory_space=pltpu.VMEM)] * 3,
        scratch_shapes=[
            pltpu.VMEM(lon_factor.shape, jnp.float32),
            pltpu.VMEM(lat_turned.shape, jnp.float32),
            pltpu.VMEM(time_factor.shape, jnp.float32),
            pltpu.SemaphoreType.DMA((3,)),
            pltpu.SemaphoreType.DMA((n_hr // LANE, n_lon // 16)),
            pltpu.VMEM((n_lat, rank, n_hr), jnp.float32),
            pltpu.VMEM((cells, rank), jnp.float32),
            pltpu.VMEM((n_lon, rank), jnp.float32),
            pltpu.VMEM(lat_factor.shape, jnp.float32),
        ] + [pltpu.VMEM((cells, LANE), jnp.float32)] * (n_hr // LANE) + comm,
        compiler_params=pltpu.CompilerParams(
            collective_id=0, has_side_effects=True, vmem_limit_bytes=52 * 1024 * 1024),
    )(flat, lon_factor, lat_turned, time_factor)
    return lon_new, lat_new.T, time_new


def solution(mesh):
    sizes = dict(mesh.shape)
    in_specs = (P("lon", "lat", "tm"), P(None, "lon"), P(None, "lat"), P(None, "tm"))
    out_specs = (P(None, "lon"), P(None, "lat"), P(None, "tm"))

    def run(*args):
        return tuple(shards(sizes, *args))

    return jax.shard_map(run, mesh=mesh, in_specs=in_specs, out_specs=out_specs, check_vma=False)
```

```python
import functools

import jax
import jax.numpy as jnp
from jax import lax
from jax.experimental import pallas as pl
from jax.experimental.pallas import tpu as pltpu
from jax.sharding import PartitionSpec as P

EPSILON = 1e-06
MESH = pl.DeviceIdType.MESH
SUB = 8
LANE = 128


def gram_of(factor):
    return lax.dot_general(
        factor, factor, (((1,), (1,)), ((), ())),
        precision=lax.Precision.HIGHEST, preferred_element_type=jnp.float32,
    )


def halves(value):
    high = value.astype(jnp.bfloat16)
    return high, (value - high.astype(jnp.float32)).astype(jnp.bfloat16)


def widen(value, rows, cols):
    r, c = value.shape
    if c < cols:
        value = jnp.concatenate([value, jnp.zeros((r, cols - c), value.dtype)], axis=1)
    if r < rows:
        value = jnp.concatenate([value, jnp.zeros((rows - r, cols), value.dtype)], axis=0)
    return value


def turn(value):
    r, c = value.shape
    full = widen(value, -(-r // LANE) * LANE, -(-c // LANE) * LANE)
    return full.T[:c, :r]


def hals(out_ref, factor, terms, gram):
    rank = factor.shape[0]
    row = lax.broadcasted_iota(jnp.int32, (rank, rank), 0)
    col = lax.broadcasted_iota(jnp.int32, (rank, rank), 1)
    inverse = 1.0 / jnp.sum(jnp.where(row == col, gram, 0.0), axis=1, keepdims=True)
    scaled = gram * inverse
    rest = (terms - jnp.dot(gram, factor, precision=lax.Precision.HIGHEST,
                            preferred_element_type=jnp.float32)) * inverse
    for r in range(rank):
        old = factor[r:r + 1]
        new = jnp.maximum(old + rest[r:r + 1], EPSILON)
        out_ref[r:r + 1, :] = new
        if r < rank - 1:
            rest = rest - scaled[:, r:r + 1] * (new - old)


def pack(value, lanes=LANE):
    rows, cols = value.shape
    blocks = max(lanes // cols, 1)
    step = rows // blocks
    return jnp.concatenate([value[i * step:(i + 1) * step] for i in range(blocks)], axis=1)


def unpack(value, cols):
    return jnp.concatenate([value[:, i:i + cols] for i in range(0, value.shape[1], cols)], axis=0)


class Group:
    def __init__(self, sizes, axes):
        self.axes = axes
        self.sizes = [sizes[a] for a in axes]
        self.count = 1
        for s in self.sizes:
            self.count *= s

    def me(self):
        index = 0
        for a, s in zip(self.axes, self.sizes):
            index = index * s + lax.axis_index(a)
        return index

    def device(self, index):
        place = {}
        for a, s in reversed(list(zip(self.axes, self.sizes))):
            place[a] = lax.rem(index, s)
            index = lax.div(index, s)
        return place

    def peer(self, offset):
        return lax.rem(self.me() + offset, self.count)

    def source(self, offset):
        return lax.rem(self.me() + (self.count - offset), self.count)


class Share:
    def __init__(self, group, slots, send, recv):
        self.group, self.slots = group, slots
        self.copies = []
        me = group.me()
        for o in range(1, group.count):
            self.copies.append(pltpu.make_async_remote_copy(
                src_ref=slots.at[me], dst_ref=slots.at[me],
                send_sem=send.at[o - 1], recv_sem=recv.at[o - 1],
                device_id=group.device(group.peer(o)), device_id_type=MESH))

    def start(self, value):
        self.slots[self.group.me()] = pack(value)
        for copy in self.copies:
            copy.start()

    def finish(self, cols):
        for copy in self.copies:
            copy.wait()
        total = self.slots[0]
        for i in range(1, self.group.count):
            total = total + self.slots[i]
        return unpack(total, cols)


class Reduce:
    def __init__(self, near, far, part, slots, across, final, *sems):
        self.near, self.far = near, far
        self.part, self.slots, self.across, self.final = part, slots, across, final
        self.per = part.shape[0] // near.count
        me, here = near.me(), far.me()
        self.scatter, self.spread, self.gather = [], [], []
        for o in range(1, near.count):
            to = near.peer(o)
            device = near.device(to)
            self.scatter.append(pltpu.make_async_remote_copy(
                src_ref=part.at[self.tiles(to)], dst_ref=slots.at[o - 1],
                send_sem=sems[0].at[o - 1], recv_sem=sems[1].at[o - 1],
                device_id=device, device_id_type=MESH))
            self.gather.append(pltpu.make_async_remote_copy(
                src_ref=final.at[self.tiles(me)], dst_ref=final.at[self.tiles(me)],
                send_sem=sems[4].at[o - 1], recv_sem=sems[5].at[o - 1],
                device_id=device, device_id_type=MESH))
        for o in range(1, far.count):
            self.spread.append(pltpu.make_async_remote_copy(
                src_ref=across.at[here], dst_ref=across.at[here],
                send_sem=sems[2].at[o - 1], recv_sem=sems[3].at[o - 1],
                device_id=far.device(far.peer(o)), device_id_type=MESH))

    def tiles(self, index):
        return pl.ds(index * self.per, self.per)

    def start(self, value):
        for i in range(value.shape[1] // LANE):
            rows = value.shape[0] // SUB
            self.part[i * rows:(i + 1) * rows] = value[:, i * LANE:(i + 1) * LANE].reshape(rows, SUB, LANE)
        for copy in self.scatter:
            copy.start()

    def middle(self):
        me = self.near.me()
        for copy in self.scatter:
            copy.wait_recv()
        total = self.part[self.tiles(me)]
        for o in range(1, self.near.count):
            total = total + self.slots[o - 1]
        self.across[self.far.me()] = total
        for copy in self.spread:
            copy.start()
        for copy in self.spread:
            copy.wait_recv()
        total = self.across[0]
        for i in range(1, self.far.count):
            total = total + self.across[i]
        self.final[self.tiles(me)] = total
        for copy in self.gather:
            copy.start()

    def finish(self, rank):
        for copy in self.gather:
            copy.wait_recv()
        rows = rank // SUB
        pieces = self.part.shape[0]
        tiles = [self.final[i:i + rows].reshape(rank, LANE) for i in range(0, pieces, rows)]
        return tiles[0] if len(tiles) == 1 else jnp.concatenate(tiles, axis=1)

    def drain(self):
        for copy in self.scatter + self.spread + self.gather:
            copy.wait_send()


def kernel(sizes, shape, x_hbm, both_hbm, lat_hbm, lon_out, lat_out, time_out,
           lon_ref, lat_ref, time_ref, load, x_load, across, inner, lon_t, lat_new_ref, *rest):
    n_lon, n_lat, n_hr = shape
    rank = lon_ref.shape[0]
    lanes = n_hr // LANE
    x_tiles, comm = rest[:lanes], rest[lanes:]
    step = 16
    chunk = step * n_lat
    small = [pltpu.make_async_copy(src, dst, load.at[i]) for i, (src, dst) in enumerate(
        ((both_hbm.at[:, pl.ds(n_lon, n_hr)], time_ref), (lat_hbm, lat_ref), (both_hbm.at[:, pl.ds(0, n_lon)], lon_ref)))]

    def piece(c):
        rows = pl.ds(pl.multiple_of(c * chunk, chunk), chunk)
        return [pltpu.make_async_copy(x_hbm.at[rows, pl.ds(t * LANE, LANE)], tile.at[rows], x_load.at[t, c])
                for t, tile in enumerate(x_tiles)]

    for copy in small:
        copy.start()
    for c in range(n_lon // step):
        for copy in piece(c):
            copy.start()
    lon_axis, lat_axis, tm_axis = (Group(sizes, (a,)) for a in ("lon", "lat", "tm"))
    lon_tm = Group(sizes, ("lon", "tm"))

    barrier = pltpu.get_barrier_semaphore()
    signals = 0
    for group in (lon_tm, lat_axis):
        for o in range(1, group.count):
            pl.semaphore_signal(barrier, inc=1, device_id=group.device(group.peer(o)), device_id_type=MESH)
            signals += 1

    for copy in small:
        copy.wait()

    lat_gram = Share(lat_axis, *comm[0:3])
    time_gram = Share(tm_axis, *comm[3:6])
    lon_gram = Share(lon_axis, *comm[6:9])
    lat_gram_new = Share(lat_axis, *comm[9:12])
    lon_sum = Reduce(tm_axis, lat_axis, *comm[12:22])
    lat_sum = Share(lon_tm, *comm[22:25])
    time_sum = Reduce(lon_axis, lat_axis, *comm[25:35])

    weights = jnp.concatenate(halves(time_ref[...]), axis=0)
    lat_t = lat_ref[...]
    lat_old = turn(lat_t)
    lat_start = gram_of(lat_old)
    time_start = gram_of(time_ref[...])

    def first(c, _):
        rows = pl.ds(pl.multiple_of(c * chunk, chunk), chunk)
        for copy in piece(c):
            copy.wait()
        high, low = halves(jnp.concatenate([tile[rows, :] for tile in x_tiles], axis=1))
        nt = (((1,), (1,)), ((), ()))
        both = lax.dot_general(high, weights, nt, preferred_element_type=jnp.float32)
        both = both + lax.dot_general(low, weights, nt, preferred_element_type=jnp.float32)
        value = both[:, :rank] + both[:, rank:]
        inner[rows, :] = value
        lon_t[pl.ds(pl.multiple_of(c * step, step), step), :] = jnp.sum(
            value.reshape(step, n_lat, rank) * lat_t[None], axis=1)
        return 0

    lax.fori_loop(0, n_lon // step, first, 0, unroll=2)
    lon_part = turn(lon_t[...])
    if signals:
        pl.semaphore_wait(barrier, signals)
    lon_sum.start(lon_part)
    lat_gram.start(lat_start)
    time_gram.start(time_start)
    lon_sum.middle()
    time_g = time_gram.finish(rank)
    gram = lat_gram.finish(rank) * time_g
    hals(lon_out, lon_ref[...], lon_sum.finish(rank), gram)

    lon_new = lon_out[...]
    lon_gram.start(gram_of(lon_new))
    lon_t[...] = turn(lon_new)

    def second(c, total):
        rows = pl.ds(pl.multiple_of(c * chunk, chunk), chunk)
        scale = lon_t[pl.ds(pl.multiple_of(c * step, step), step), :]
        return total + jnp.sum(inner[rows, :].reshape(step, n_lat, rank) * scale[:, None, :], axis=0)

    lat_part = lax.fori_loop(0, n_lon // step, second, jnp.zeros((n_lat, rank), jnp.float32), unroll=2)
    lat_sum.start(turn(lat_part))

    lon_halves = jnp.concatenate(halves(lon_new), axis=0)

    def third(j, _):
        plane = jnp.concatenate(
            [tile[pl.ds(j, n_lon, stride=n_lat), :] for tile in x_tiles], axis=1)
        high, low = halves(plane)
        both = jnp.dot(lon_halves, high, preferred_element_type=jnp.float32)
        both = both + jnp.dot(lon_halves, low, preferred_element_type=jnp.float32)
        across[j] = both[:rank] + both[rank:]
        return 0

    lax.fori_loop(0, n_lat, third, 0, unroll=2)
    lon_g = lon_gram.finish(rank)
    gram = lon_g * time_g
    hals(lat_new_ref, lat_old, lat_sum.finish(n_lat), gram)

    lat_new = lat_new_ref[...]
    lat_gram_new.start(gram_of(lat_new))

    time_part = across[0] * lat_new[:, 0:1]
    for j in range(1, n_lat):
        time_part = time_part + across[j] * lat_new[:, j:j + 1]
    time_sum.start(time_part)
    time_sum.middle()
    gram = lon_g * lat_gram_new.finish(rank)
    lat_out[...] = turn(lat_new)
    hals(time_out, time_ref[...], time_sum.finish(rank), gram)
    for part in (lon_sum, time_sum):
        part.drain()


def shards(sizes, reanalysis, lon_factor, lat_factor, time_factor):
    n_lon, n_lat, n_hr = reanalysis.shape
    rank = lon_factor.shape[0]
    cells = n_lon * n_lat
    flat = reanalysis.reshape(cells, n_hr)

    def sems(count):
        return [pltpu.SemaphoreType.DMA((max(count - 1, 1),))] * 2

    def share(count, columns=rank):
        blocks = max(LANE // columns, 1)
        return [pltpu.VMEM((count, rank // blocks, blocks * columns), jnp.float32)] + sems(count)

    def reduce(near, far, columns):
        pieces = rank // SUB * -(-columns // LANE)
        per = pieces // near
        return [
            pltpu.VMEM((pieces, SUB, LANE), jnp.float32),
            pltpu.VMEM((max(near - 1, 1), per, SUB, LANE), jnp.float32),
            pltpu.VMEM((far, per, SUB, LANE), jnp.float32),
            pltpu.VMEM((pieces, SUB, LANE), jnp.float32),
        ] + sems(near) + sems(far) + sems(near)

    lon, lat, tm = sizes["lon"], sizes["lat"], sizes["tm"]
    comm = share(lat) + share(tm) + share(lon) + share(lat)
    comm += reduce(tm, lat, n_lon) + share(lon * tm, n_lat) + reduce(lon, lat, n_hr)
    lat_turned = lat_factor.T
    lon_new, lat_new, time_new = pl.pallas_call(
        functools.partial(kernel, sizes, (n_lon, n_lat, n_hr)),
        out_shape=[jax.ShapeDtypeStruct(f.shape, jnp.float32) for f in (lon_factor, lat_turned, time_factor)],
        in_specs=[pl.BlockSpec(memory_space=pltpu.HBM)] * 3,
        out_specs=[pl.BlockSpec(memory_space=pltpu.VMEM)] * 3,
        scratch_shapes=[
            pltpu.VMEM(lon_factor.shape, jnp.float32),
            pltpu.VMEM(lat_turned.shape, jnp.float32),
            pltpu.VMEM(time_factor.shape, jnp.float32),
            pltpu.SemaphoreType.DMA((3,)),
            pltpu.SemaphoreType.DMA((n_hr // LANE, n_lon // 16)),
            pltpu.VMEM((n_lat, rank, n_hr), jnp.float32),
            pltpu.VMEM((cells, rank), jnp.float32),
            pltpu.VMEM((n_lon, rank), jnp.float32),
            pltpu.VMEM(lat_factor.shape, jnp.float32),
        ] + [pltpu.VMEM((cells, LANE), jnp.float32)] * (n_hr // LANE) + comm,
        compiler_params=pltpu.CompilerParams(
            collective_id=0, has_side_effects=True, vmem_limit_bytes=52 * 1024 * 1024),
    )(flat, jnp.concatenate([lon_factor, time_factor], axis=1), lat_turned)
    return lon_new, lat_new.T, time_new


def solution(mesh):
    sizes = dict(mesh.shape)
    in_specs = (P("lon", "lat", "tm"), P(None, "lon"), P(None, "lat"), P(None, "tm"))
    out_specs = (P(None, "lon"), P(None, "lat"), P(None, "tm"))

    def run(*args):
        return tuple(shards(sizes, *args))

    return jax.shard_map(run, mesh=mesh, in_specs=in_specs, out_specs=out_specs, check_vma=False)
```

```python
import functools

import jax
import jax.numpy as jnp
from jax import lax
from jax.experimental import pallas as pl
from jax.experimental.pallas import tpu as pltpu
from jax.sharding import PartitionSpec as P

EPSILON = 1e-06
MESH = pl.DeviceIdType.MESH
SUB = 8
LANE = 128


def gram_of(factor):
    return lax.dot_general(
        factor, factor, (((1,), (1,)), ((), ())),
        precision=lax.Precision.HIGHEST, preferred_element_type=jnp.float32,
    )


def halves(value):
    high = value.astype(jnp.bfloat16)
    return high, (value - high.astype(jnp.float32)).astype(jnp.bfloat16)


def widen(value, rows, cols):
    r, c = value.shape
    if c < cols:
        value = jnp.concatenate([value, jnp.zeros((r, cols - c), value.dtype)], axis=1)
    if r < rows:
        value = jnp.concatenate([value, jnp.zeros((rows - r, cols), value.dtype)], axis=0)
    return value


def turn(value):
    r, c = value.shape
    full = widen(value, -(-r // LANE) * LANE, -(-c // LANE) * LANE)
    return full.T[:c, :r]


def hals(out_ref, factor, terms, gram):
    rank = factor.shape[0]
    row = lax.broadcasted_iota(jnp.int32, (rank, rank), 0)
    col = lax.broadcasted_iota(jnp.int32, (rank, rank), 1)
    inverse = 1.0 / jnp.sum(jnp.where(row == col, gram, 0.0), axis=1, keepdims=True)
    scaled = gram * inverse
    rest = (terms - jnp.dot(gram, factor, precision=lax.Precision.HIGHEST,
                            preferred_element_type=jnp.float32)) * inverse
    for r in range(rank):
        old = factor[r:r + 1]
        new = jnp.maximum(old + rest[r:r + 1], EPSILON)
        out_ref[r:r + 1, :] = new
        if r < rank - 1:
            rest = rest - scaled[:, r:r + 1] * (new - old)


def pack(value, lanes=LANE):
    rows, cols = value.shape
    blocks = max(lanes // cols, 1)
    step = rows // blocks
    return jnp.concatenate([value[i * step:(i + 1) * step] for i in range(blocks)], axis=1)


def unpack(value, cols):
    return jnp.concatenate([value[:, i:i + cols] for i in range(0, value.shape[1], cols)], axis=0)


class Group:
    def __init__(self, sizes, axes):
        self.axes = axes
        self.sizes = [sizes[a] for a in axes]
        self.count = 1
        for s in self.sizes:
            self.count *= s

    def me(self):
        index = 0
        for a, s in zip(self.axes, self.sizes):
            index = index * s + lax.axis_index(a)
        return index

    def device(self, index):
        place = {}
        for a, s in reversed(list(zip(self.axes, self.sizes))):
            place[a] = lax.rem(index, s)
            index = lax.div(index, s)
        return place

    def peer(self, offset):
        return lax.rem(self.me() + offset, self.count)

    def source(self, offset):
        return lax.rem(self.me() + (self.count - offset), self.count)


class Share:
    def __init__(self, group, slots, send, recv):
        self.group, self.slots = group, slots
        self.copies = []
        me = group.me()
        for o in range(1, group.count):
            self.copies.append(pltpu.make_async_remote_copy(
                src_ref=slots.at[me], dst_ref=slots.at[me],
                send_sem=send.at[o - 1], recv_sem=recv.at[o - 1],
                device_id=group.device(group.peer(o)), device_id_type=MESH))

    def start(self, value):
        self.slots[self.group.me()] = pack(value)
        for copy in self.copies:
            copy.start()

    def finish(self, cols):
        for copy in self.copies:
            copy.wait()
        total = self.slots[0]
        for i in range(1, self.group.count):
            total = total + self.slots[i]
        return unpack(total, cols)


class Reduce:
    def __init__(self, near, far, part, slots, across, final, *sems):
        self.near, self.far = near, far
        self.part, self.slots, self.across, self.final = part, slots, across, final
        self.per = part.shape[0] // near.count
        me, here = near.me(), far.me()
        self.scatter, self.spread, self.gather = [], [], []
        for o in range(1, near.count):
            to = near.peer(o)
            device = near.device(to)
            self.scatter.append(pltpu.make_async_remote_copy(
                src_ref=part.at[self.tiles(to)], dst_ref=slots.at[o - 1],
                send_sem=sems[0].at[o - 1], recv_sem=sems[1].at[o - 1],
                device_id=device, device_id_type=MESH))
            self.gather.append(pltpu.make_async_remote_copy(
                src_ref=final.at[self.tiles(me)], dst_ref=final.at[self.tiles(me)],
                send_sem=sems[4].at[o - 1], recv_sem=sems[5].at[o - 1],
                device_id=device, device_id_type=MESH))
        for o in range(1, far.count):
            self.spread.append(pltpu.make_async_remote_copy(
                src_ref=across.at[here], dst_ref=across.at[here],
                send_sem=sems[2].at[o - 1], recv_sem=sems[3].at[o - 1],
                device_id=far.device(far.peer(o)), device_id_type=MESH))

    def tiles(self, index):
        return pl.ds(index * self.per, self.per)

    def start(self, value):
        for i in range(value.shape[1] // LANE):
            rows = value.shape[0] // SUB
            self.part[i * rows:(i + 1) * rows] = value[:, i * LANE:(i + 1) * LANE].reshape(rows, SUB, LANE)
        for copy in self.scatter:
            copy.start()

    def middle(self):
        me = self.near.me()
        for copy in self.scatter:
            copy.wait_recv()
        total = self.part[self.tiles(me)]
        for o in range(1, self.near.count):
            total = total + self.slots[o - 1]
        self.across[self.far.me()] = total
        for copy in self.spread:
            copy.start()
        for copy in self.spread:
            copy.wait_recv()
        total = self.across[0]
        for i in range(1, self.far.count):
            total = total + self.across[i]
        self.final[self.tiles(me)] = total
        for copy in self.gather:
            copy.start()

    def finish(self, rank):
        for copy in self.gather:
            copy.wait_recv()
        rows = rank // SUB
        pieces = self.part.shape[0]
        tiles = [self.final[i:i + rows].reshape(rank, LANE) for i in range(0, pieces, rows)]
        return tiles[0] if len(tiles) == 1 else jnp.concatenate(tiles, axis=1)

    def drain(self):
        for copy in self.scatter + self.spread + self.gather:
            copy.wait_send()


def kernel(sizes, shape, x_hbm, both_hbm, lat_hbm, lon_out, lat_out, time_out,
           lon_ref, lat_ref, time_ref, load, x_load, across, inner, lon_t, lat_new_ref, *rest):
    n_lon, n_lat, n_hr = shape
    rank = lon_ref.shape[0]
    lanes = n_hr // LANE
    x_tiles, comm = rest[:lanes], rest[lanes:]
    step = 16
    chunk = step * n_lat
    small = [pltpu.make_async_copy(src, dst, load.at[i]) for i, (src, dst) in enumerate(
        ((both_hbm.at[:, pl.ds(n_lon, n_hr)], time_ref), (lat_hbm, lat_ref), (both_hbm.at[:, pl.ds(0, n_lon)], lon_ref)))]

    def piece(c):
        rows = pl.ds(pl.multiple_of(c * chunk, chunk), chunk)
        return [pltpu.make_async_copy(x_hbm.at[rows, pl.ds(t * LANE, LANE)], tile.at[rows], x_load.at[t, c])
                for t, tile in enumerate(x_tiles)]

    for copy in small:
        copy.start()
    for c in range(n_lon // step):
        for copy in piece(c):
            copy.start()
    lon_axis, lat_axis, tm_axis = (Group(sizes, (a,)) for a in ("lon", "lat", "tm"))
    lon_tm = Group(sizes, ("lon", "tm"))

    barrier = pltpu.get_barrier_semaphore()
    signals = 0
    for group in (lon_tm, lat_axis):
        for o in range(1, group.count):
            pl.semaphore_signal(barrier, inc=1, device_id=group.device(group.peer(o)), device_id_type=MESH)
            signals += 1

    for copy in small:
        copy.wait()

    lat_gram = Share(lat_axis, *comm[0:3])
    time_gram = Share(tm_axis, *comm[3:6])
    lon_gram = Share(lon_axis, *comm[6:9])
    lat_gram_new = Share(lat_axis, *comm[9:12])
    lon_sum = Reduce(tm_axis, lat_axis, *comm[12:22])
    lat_sum = Share(lon_tm, *comm[22:25])
    time_sum = Reduce(lon_axis, lat_axis, *comm[25:35])

    weights = jnp.concatenate(halves(time_ref[...]), axis=0)
    lat_t = lat_ref[...]
    lat_old = turn(lat_t)
    lat_start = gram_of(lat_old)
    time_start = gram_of(time_ref[...])

    def first(c, _):
        rows = pl.ds(pl.multiple_of(c * chunk, chunk), chunk)
        for copy in piece(c):
            copy.wait()
        high, low = halves(jnp.concatenate([tile[rows, :] for tile in x_tiles], axis=1))
        nt = (((1,), (1,)), ((), ()))
        both = lax.dot_general(high, weights, nt, preferred_element_type=jnp.float32)
        both = both + lax.dot_general(low, weights, nt, preferred_element_type=jnp.float32)
        value = both[:, :rank] + both[:, rank:]
        inner[rows, :] = value
        lon_t[pl.ds(pl.multiple_of(c * step, step), step), :] = jnp.sum(
            value.reshape(step, n_lat, rank) * lat_t[None], axis=1)
        return 0

    lax.fori_loop(0, n_lon // step, first, 0, unroll=4)
    lon_part = turn(lon_t[...])
    if signals:
        pl.semaphore_wait(barrier, signals)
    lon_sum.start(lon_part)
    lat_gram.start(lat_start)
    time_gram.start(time_start)
    lon_sum.middle()
    time_g = time_gram.finish(rank)
    gram = lat_gram.finish(rank) * time_g
    hals(lon_out, lon_ref[...], lon_sum.finish(rank), gram)

    lon_new = lon_out[...]
    lon_gram.start(gram_of(lon_new))
    lon_t[...] = turn(lon_new)

    def second(c, total):
        rows = pl.ds(pl.multiple_of(c * chunk, chunk), chunk)
        scale = lon_t[pl.ds(pl.multiple_of(c * step, step), step), :]
        return total + jnp.sum(inner[rows, :].reshape(step, n_lat, rank) * scale[:, None, :], axis=0)

    lat_part = lax.fori_loop(0, n_lon // step, second, jnp.zeros((n_lat, rank), jnp.float32), unroll=4)
    lat_sum.start(turn(lat_part))

    lon_halves = jnp.concatenate(halves(lon_new), axis=0)

    def third(j, _):
        plane = jnp.concatenate(
            [tile[pl.ds(j, n_lon, stride=n_lat), :] for tile in x_tiles], axis=1)
        high, low = halves(plane)
        both = jnp.dot(lon_halves, high, preferred_element_type=jnp.float32)
        both = both + jnp.dot(lon_halves, low, preferred_element_type=jnp.float32)
        across[j] = both[:rank] + both[rank:]
        return 0

    lax.fori_loop(0, n_lat, third, 0, unroll=4)
    lon_g = lon_gram.finish(rank)
    gram = lon_g * time_g
    hals(lat_new_ref, lat_old, lat_sum.finish(n_lat), gram)

    lat_new = lat_new_ref[...]
    lat_gram_new.start(gram_of(lat_new))

    time_part = across[0] * lat_new[:, 0:1]
    for j in range(1, n_lat):
        time_part = time_part + across[j] * lat_new[:, j:j + 1]
    time_sum.start(time_part)
    time_sum.middle()
    gram = lon_g * lat_gram_new.finish(rank)
    lat_out[...] = turn(lat_new)
    hals(time_out, time_ref[...], time_sum.finish(rank), gram)
    for part in (lon_sum, time_sum):
        part.drain()


def shards(sizes, reanalysis, lon_factor, lat_factor, time_factor):
    n_lon, n_lat, n_hr = reanalysis.shape
    rank = lon_factor.shape[0]
    cells = n_lon * n_lat
    flat = reanalysis.reshape(cells, n_hr)

    def sems(count):
        return [pltpu.SemaphoreType.DMA((max(count - 1, 1),))] * 2

    def share(count, columns=rank):
        blocks = max(LANE // columns, 1)
        return [pltpu.VMEM((count, rank // blocks, blocks * columns), jnp.float32)] + sems(count)

    def reduce(near, far, columns):
        pieces = rank // SUB * -(-columns // LANE)
        per = pieces // near
        return [
            pltpu.VMEM((pieces, SUB, LANE), jnp.float32),
            pltpu.VMEM((max(near - 1, 1), per, SUB, LANE), jnp.float32),
            pltpu.VMEM((far, per, SUB, LANE), jnp.float32),
            pltpu.VMEM((pieces, SUB, LANE), jnp.float32),
        ] + sems(near) + sems(far) + sems(near)

    lon, lat, tm = sizes["lon"], sizes["lat"], sizes["tm"]
    comm = share(lat) + share(tm) + share(lon) + share(lat)
    comm += reduce(tm, lat, n_lon) + share(lon * tm, n_lat) + reduce(lon, lat, n_hr)
    lat_turned = lat_factor.T
    lon_new, lat_new, time_new = pl.pallas_call(
        functools.partial(kernel, sizes, (n_lon, n_lat, n_hr)),
        out_shape=[jax.ShapeDtypeStruct(f.shape, jnp.float32) for f in (lon_factor, lat_turned, time_factor)],
        in_specs=[pl.BlockSpec(memory_space=pltpu.HBM)] * 3,
        out_specs=[pl.BlockSpec(memory_space=pltpu.VMEM)] * 3,
        scratch_shapes=[
            pltpu.VMEM(lon_factor.shape, jnp.float32),
            pltpu.VMEM(lat_turned.shape, jnp.float32),
            pltpu.VMEM(time_factor.shape, jnp.float32),
            pltpu.SemaphoreType.DMA((3,)),
            pltpu.SemaphoreType.DMA((n_hr // LANE, n_lon // 16)),
            pltpu.VMEM((n_lat, rank, n_hr), jnp.float32),
            pltpu.VMEM((cells, rank), jnp.float32),
            pltpu.VMEM((n_lon, rank), jnp.float32),
            pltpu.VMEM(lat_factor.shape, jnp.float32),
        ] + [pltpu.VMEM((cells, LANE), jnp.float32)] * (n_hr // LANE) + comm,
        compiler_params=pltpu.CompilerParams(
            collective_id=0, has_side_effects=True, vmem_limit_bytes=52 * 1024 * 1024),
    )(flat, jnp.concatenate([lon_factor, time_factor], axis=1), lat_turned)
    return lon_new, lat_new.T, time_new


def solution(mesh):
    sizes = dict(mesh.shape)
    in_specs = (P("lon", "lat", "tm"), P(None, "lon"), P(None, "lat"), P(None, "tm"))
    out_specs = (P(None, "lon"), P(None, "lat"), P(None, "tm"))

    def run(*args):
        return tuple(shards(sizes, *args))

    return jax.shard_map(run, mesh=mesh, in_specs=in_specs, out_specs=out_specs, check_vma=False)
```
